128 devices in a mesh: tm: 4 (over x), vox: 32 (over y, z, core).
Axes of the slice: x: 4, y: 4, z: 4, core: 2. Of those that a mesh axis runs over, the one named last changes fastest.
Arguments:
- u_train: bfloat16 [3072, 4096], P('tm'), may hold values from -0.109375 to 0.109375
- y_train: bfloat16 [3072, 12288], P('tm', 'vox'), may hold values from -6 to 6
- sing: float32 [4096], replicated, may hold values from 0.5 to 8
- lambdas: float32 [20], replicated, may hold values from 0.1 to 100
- lam_index: int32 [96], P('vox'), may hold values from 0 to 19
- live: int32 [96], P('vox'), may hold values from 0 to 1, as said below
- v_basis: bfloat16 [4096, 4096], P('tm', 'vox'), may hold values from -0.09375 to 0.09375
- x_test: bfloat16 [1024, 4096], P(None, 'tm'), may hold values from -0.09375 to 0.09375
Outputs:
- weights: bfloat16 [4096, 12288], P('tm', 'vox')
- predictions: bfloat16 [1024, 12288], P('tm', 'vox')
The draws below stay inside these ranges and needn't reach their ends.
Inputs may be any that keep to these rules, and one draw needn't show every extreme that they name: Of the 3 voxel blocks that one device along vox holds, at most 2 are live, and some device holds exactly 2.
All inputs are finite; a program needn't handle non-finite values.
Results may differ from the reference program's by a relative error of at most 0.0058.
Values may be sent and summed in bfloat16 or wider, within the bound.
No kernel may reach another device: no remote copies, remote signals or barrier semaphores. Data moves between devices by JAX's collectives and lax.ppermute only.
A program may use at most 128 MiB of HBM per device.

```python
import math
import jax
import jax.numpy as jnp

F = 4096
NLAM = 20
BLK = 128
VD = 384
TEST = 1024
TR = 3072
VOX = 12288
NBLK = 96


def draw_live(key, part):
    block_count = VD // BLK
    device_count = NBLK // block_count
    capacity = block_count - block_count // 3
    first_key = jax.random.fold_in(key, 11)
    second_key = jax.random.fold_in(key, 12)
    third_key = jax.random.fold_in(key, 13)
    counts = jax.random.randint(first_key, (device_count,), 1, capacity + 1)
    fullest = jax.random.randint(second_key, (), 0, device_count)
    counts = jnp.where(jnp.arange(device_count) == fullest, capacity, counts)
    scores = jax.random.randint(third_key, (device_count, block_count), 0, 1 << 20)
    scores = scores * block_count + jnp.arange(block_count)[None, :]
    ranking = jnp.argsort(jnp.argsort(scores, axis=1), axis=1)
    marked = (ranking < counts[:, None]).astype(jnp.int32)
    return marked.reshape(NBLK)


def plant(values, rng, least, top_value):
    extent = values.shape
    place = [jax.random.randint(jax.random.fold_in(rng, axis), (), 0, extent[axis]) for axis in range(len(extent))]
    values = values.at[tuple(place)].set(least)
    longest = extent.index(max(extent))
    place[longest] = (place[longest] + 1) % extent[longest]
    return values.at[tuple(place)].set(top_value)


def block_levels(key, extent, cuts, low, top_value):
    gain = 1.0
    for position, shards_of in cuts:
        steps = jax.random.uniform(jax.random.fold_in(jax.random.fold_in(key, 6), position), (shards_of,), jnp.float32, low / len(cuts), top_value / len(cuts))
        gain = gain * jnp.repeat(jnp.exp(steps), extent[position] // shards_of).reshape((-1,) + (1,) * (len(extent) - 1 - position))
    return gain


def centred(stream_key, dims, deviation, bound, cuts=(), kind=jnp.bfloat16):
    result = deviation * jax.random.normal(stream_key, dims, jnp.float32)
    if cuts:
        result = result * block_levels(stream_key, dims, cuts, -0.22, 0.18)
    return jnp.clip(result, -bound, bound).astype(kind)


def setup_inputs(seed: int = 0) -> dict:
    key_list = jax.random.split(jax.random.key(seed), 9)
    u_train = centred(key_list[0], (TR, F), TR ** -0.5, 0.109375, ((0, 4),))
    y_train = centred(key_list[1], (TR, VOX), 1.0, 6.0, ((0, 4), (1, 32)))
    sing = jnp.clip(jnp.exp(jax.random.uniform(key_list[2], (F,), jnp.float32, math.log(0.5), math.log(8.0))), 0.5, 8.0)
    lambdas = jnp.clip(jnp.exp(jax.random.uniform(key_list[3], (NLAM,), jnp.float32, math.log(0.1), math.log(100.0))), 0.1, 100.0)
    lam_index = plant(jax.random.randint(key_list[4], (NBLK,), 0, NLAM), jax.random.fold_in(key_list[4], 1), 0, NLAM - 1).astype(jnp.int32)
    live = draw_live(jax.random.fold_in(key_list[8], 71), 0)
    v_basis = centred(key_list[6], (F, F), F ** -0.5, 0.09375, ((0, 4), (1, 32)))
    x_test = centred(key_list[7], (TEST, F), F ** -0.5, 0.09375, ((1, 4),))
    return dict(u_train=u_train, y_train=y_train, sing=sing, lambdas=lambdas, lam_index=lam_index, live=live, v_basis=v_basis, x_test=x_test)


def reference(u_train, y_train, sing, lambdas, lam_index, live, v_basis, x_test):
    filters = sing[None, :] / (sing[None, :] * sing[None, :] + lambdas[:, None])
    products = jnp.dot(u_train.T, y_train, preferred_element_type=jnp.float32)
    chosen = filters[lam_index] * live[:, None].astype(jnp.float32)
    blocks = products.reshape(F, NBLK, BLK) * chosen.T[:, :, None]
    filtered = blocks.reshape(F, VOX).astype(jnp.bfloat16)
    weights = jnp.dot(v_basis, filtered, preferred_element_type=jnp.float32).astype(jnp.bfloat16)
    predictions = jnp.dot(x_test, weights, preferred_element_type=jnp.float32).astype(jnp.bfloat16)
    return weights, predictions
```

```python
import functools

import jax
import jax.numpy as jnp
from jax import lax
from jax.experimental import pallas as pl
from jax.experimental.pallas import tpu as pltpu
from jax.sharding import PartitionSpec as P

F32 = jnp.float32
BF16 = jnp.bfloat16
F = 4096
NLAM = 20
BLK = 128
VD = 384
NB = 3
NS = 2
TEST = 1024
T = 768
Q = 1024
W = NS * BLK
NX = NY = NZ = 4
NC = 2
SMEM = pl.BlockSpec(memory_space=pltpu.SMEM)
VMEM = pl.BlockSpec(memory_space=pltpu.VMEM)
ANY = pl.BlockSpec(memory_space=pl.ANY)


def moves(target):
    pairs = []
    for x in range(NX):
        for y in range(NY):
            for z in range(NZ):
                for c in range(NC):
                    tx, ty, tz, tc = target(x, y, z, c)
                    source = ((x * NY + y) * NZ + z) * NC + c
                    goal = (((tx % NX) * NY + ty % NY) * NZ + tz % NZ) * NC + tc % NC
                    pairs.append((source, goal))
    return pairs


PRIMARY = moves(lambda x, y, z, c: (x + 1 - 2 * c, y, z, c))
SECONDARY = moves(lambda x, y, z, c: (x - 1 + 2 * c, y, z, c))
OPPOSITE = moves(lambda x, y, z, c: (x + 2, y, z, c))
SWAP = moves(lambda x, y, z, c: (x, y, z, c + 1))
FIRST = [moves(lambda x, y, z, c, d=d: (x, y + d * (1 - c), z + d * c, c)) for d in (1, 2, 3)]
SECOND = [moves(lambda x, y, z, c, d=d: (x, y + d * c, z + d * (1 - c), c)) for d in (1, 2, 3)]


def send(value, pairs):
    return lax.ppermute(value, ("tm", "vox"), pairs)


def place():
    x = lax.axis_index("tm")
    v = lax.axis_index("vox")
    return x, v // (NZ * NC), (v // NC) % NZ, v % NC


def slots(live):
    first = jnp.where(live[0] > 0, 0, jnp.where(live[1] > 0, 1, 2))
    second = jnp.where(live[2] > 0, 2, jnp.where(live[1] > 0, 1, 0))
    return first, second


def quarter(which, x, c):
    step = 1 - 2 * c
    if which == "primary":
        return (x + step + NX) % NX
    if which == "secondary":
        return (x - step + NX) % NX
    if which == "opposite":
        return (x + 2) % NX
    return x


def partial_kernel(which, lambdas, lam_index, live, sing, u, y, *rest):
    n = len(which)
    outs, (ys, us, sems) = rest[:n], rest[n:]
    x, _, _, c = place()
    picked = slots(live)
    copies = []
    for i, slot in enumerate(picked):
        source = y.at[:, pl.ds(pl.multiple_of(slot * BLK, BLK), BLK)]
        copies.append(pltpu.make_async_copy(source, ys.at[i], sems.at[i]))
    where = [quarter(name, x, c) for name in which]
    for i, q in enumerate(where):
        source = u.at[:, pl.ds(pl.multiple_of(q * Q, Q), Q)]
        copies.append(pltpu.make_async_copy(source, us.at[i], sems.at[NS + i]))
    for copy in copies:
        copy.start()
    copies[0].wait()
    copies[1].wait()
    yt = jnp.concatenate([ys[0], ys[1]], axis=1).T
    for i, q in enumerate(where):
        copies[NS + i].wait()
        total = jnp.dot(yt, us[i], preferred_element_type=F32)
        s = sing[:, pl.ds(pl.multiple_of(q * Q, Q), Q)]
        for j, slot in enumerate(picked):
            scale = s / (s * s + lambdas[lam_index[slot]]) * live[slot].astype(F32)
            rows = slice(j * BLK, (j + 1) * BLK)
            outs[i][rows, :] = (total[rows, :] * scale).astype(outs[i].dtype)


def partial_call(which, dtypes, lambdas, lam_index, live, sing, u, y):
    n = len(which)
    return pl.pallas_call(
        functools.partial(partial_kernel, which),
        out_shape=[jax.ShapeDtypeStruct((W, Q), d) for d in dtypes],
        in_specs=[SMEM, SMEM, SMEM, VMEM, ANY, ANY],
        out_specs=[VMEM] * n,
        scratch_shapes=[
            pltpu.VMEM((NS, T, BLK), BF16),
            pltpu.VMEM((n, T, Q), BF16),
            pltpu.SemaphoreType.DMA((NS + n,)),
        ],
        compiler_params=pltpu.CompilerParams(vmem_limit_bytes=24 << 20),
        cost_estimate=pl.CostEstimate(
            flops=2 * W * T * Q * n, bytes_accessed=2 * T * Q * n + 4 * W * Q * n, transcendentals=0
        ),
    )(lambdas, lam_index, live, sing, u, y)


def shard_copies(q, slot, own, other, held, sems):
    _, y, z, c = place()
    back = (y - q + NY) % NY
    found = []
    for core in range(NC):
        for same in range(2):
            blocks = own if same else other
            mine = (c == core) if same else (c != core)
            for k in range(NZ):
                at = (slot * NZ + (z - k + NZ) % NZ) * NC + core
                if core == 0:
                    copy = pltpu.make_async_copy(blocks[k].at[back], held.at[at], sems.at[at])
                    found.append((mine, copy))
                else:
                    for i in range(NY):
                        copy = pltpu.make_async_copy(blocks[i].at[k], held.at[at], sems.at[at])
                        found.append((mine & (back == i), copy))
    return found


def start_all(found):
    for condition, copy in found:
        pl.when(condition)(copy.start)


def wait_shards(slot, own, held, sems):
    for i in range(NZ * NC):
        at = slot * NZ * NC + i
        pltpu.make_async_copy(own[0].at[0], held.at[at], sems.at[at]).wait()


def multiply(slot, held, features):
    total = None
    for z in range(NZ):
        at = slot * NZ * NC + z * NC
        left = jnp.concatenate([held[at], held[at + 1]], axis=1)
        right = features[:, z * NC * BLK : (z + 1) * NC * BLK]
        part = lax.dot_general(left, right, (((1,), (1,)), ((), ())), preferred_element_type=F32)
        total = part if total is None else total + part
    return total


def three_kernel(*refs):
    own, other, features = refs[:4], refs[4:8], refs[8:11]
    out, held, sems = refs[11:]
    x, _, _, c = place()
    names = ("own", "primary", "secondary")
    for i, name in enumerate(names):
        start_all(shard_copies(quarter(name, x, c), i, own, other, held, sems))
    for i in range(3):
        wait_shards(i, own, held, sems)
        part = multiply(i, held, features[i])
        if i == 0:
            out[...] = part
        else:
            out[...] += part


def three_call(own, other, features):
    return pl.pallas_call(
        three_kernel,
        out_shape=jax.ShapeDtypeStruct((Q, W), F32),
        in_specs=[ANY] * 8 + [VMEM] * 3,
        out_specs=VMEM,
        scratch_shapes=[
            pltpu.VMEM((3 * NZ * NC, Q, BLK), BF16),
            pltpu.SemaphoreType.DMA((3 * NZ * NC,)),
        ],
        compiler_params=pltpu.CompilerParams(vmem_limit_bytes=32 << 20),
        cost_estimate=pl.CostEstimate(
            flops=2 * W * 3 * Q * Q, bytes_accessed=2 * Q * 3 * Q, transcendentals=0
        ),
    )(*own, *other, *features)


def spread(out, values, live):
    first, second = slots(live)
    left, right = values[:, :BLK], values[:, BLK:]
    for b in range(NB):
        alive = live[b] > 0
        block = jnp.where(first == b, left, right)
        out[:, b * BLK : (b + 1) * BLK] = jnp.where(alive, block, jnp.zeros_like(block)).astype(
            out.dtype
        )


def last_kernel(live, *refs):
    own, other = refs[:4], refs[4:8]
    features, so_far, tests = refs[8:11]
    weights, mine, primary, secondary, opposite, held, sems = refs[11:]
    x, _, _, c = place()
    start_all(shard_copies(quarter("opposite", x, c), 0, own, other, held, sems))
    wait_shards(0, own, held, sems)
    total = (so_far[...] + multiply(0, held, features)).astype(BF16)
    spread(weights, total, live)
    rows = TEST // NX
    for name, out in (
        ("opposite", opposite),
        ("primary", primary),
        ("secondary", secondary),
        ("own", mine),
    ):
        q = quarter(name, x, c)
        part = tests[pl.ds(pl.multiple_of(q * rows, rows), rows), :]
        out[...] = jnp.dot(part, total, preferred_element_type=F32).astype(out.dtype)


def last_call(live, own, other, features, so_far, tests):
    rows = TEST // NX
    return pl.pallas_call(
        last_kernel,
        out_shape=[
            jax.ShapeDtypeStruct((Q, VD), BF16),
            jax.ShapeDtypeStruct((rows, W), F32),
            jax.ShapeDtypeStruct((rows, W), BF16),
            jax.ShapeDtypeStruct((rows, W), BF16),
            jax.ShapeDtypeStruct((rows, W), BF16),
        ],
        in_specs=[SMEM] + [ANY] * 8 + [VMEM] * 3,
        out_specs=[VMEM] * 5,
        scratch_shapes=[
            pltpu.VMEM((NZ * NC, Q, BLK), BF16),
            pltpu.SemaphoreType.DMA((NZ * NC,)),
        ],
        compiler_params=pltpu.CompilerParams(vmem_limit_bytes=32 << 20),
        cost_estimate=pl.CostEstimate(
            flops=4 * W * Q * Q, bytes_accessed=4 * Q * Q, transcendentals=0
        ),
    )(live, *own, *other, features, so_far, tests)


def end_kernel(live, mine, a, b, c, out):
    total = mine[...] + a[...].astype(F32) + b[...].astype(F32) + c[...].astype(F32)
    spread(out, total.astype(BF16), live)


def end_call(live, mine, a, b, c):
    return pl.pallas_call(
        end_kernel,
        out_shape=jax.ShapeDtypeStruct((TEST // NX, VD), BF16),
        in_specs=[SMEM] + [VMEM] * 4,
        out_specs=VMEM,
    )(live, mine, a, b, c)


def body(u_train, y_train, sing, lambdas, lam_index, live, v_basis, x_test):
    sing = sing.reshape(1, F)
    small = (lambdas, lam_index, live, sing, u_train, y_train)
    near = [send(v_basis, pairs) for pairs in FIRST]
    (p_opposite,) = partial_call(("opposite",), (BF16,), *small)
    come = send(p_opposite, PRIMARY)
    p_primary, p_secondary, p_own = partial_call(
        ("primary", "secondary", "own"), (F32, BF16, F32), *small
    )
    row = jnp.stack([v_basis, *near])
    own = [row] + [send(row, pairs) for pairs in SECOND]
    other = [send(block, SWAP) for block in own]
    onward = (p_primary + come.astype(F32)).astype(BF16)
    from_secondary = send(onward, PRIMARY)
    from_primary = send(p_secondary, SECONDARY)
    filtered = (p_own + from_secondary.astype(F32) + from_primary.astype(F32)).astype(BF16)
    f_secondary = send(filtered, PRIMARY)
    f_primary = send(filtered, SECONDARY)
    f_opposite = send(f_secondary, PRIMARY)
    so_far = three_call(own, other, (filtered, f_primary, f_secondary))
    weights, mine, primary, secondary, opposite = last_call(
        live, own, other, f_opposite, so_far, x_test
    )
    predictions = end_call(
        live, mine, send(opposite, OPPOSITE), send(primary, PRIMARY), send(secondary, SECONDARY)
    )
    return weights, predictions


def solution(mesh):
    placed = (
        P("tm", None),
        P("tm", "vox"),
        P(),
        P(),
        P("vox"),
        P("vox"),
        P("tm", "vox"),
        P(None, "tm"),
    )
    return jax.shard_map(
        body,
        mesh=mesh,
        in_specs=placed,
        out_specs=(P("tm", "vox"), P("tm", "vox")),
        check_vma=False,
    )
```

```python
import functools

import jax
import jax.numpy as jnp
from jax import lax
from jax.experimental import pallas as pl
from jax.experimental.pallas import tpu as pltpu
from jax.sharding import PartitionSpec as P

F32 = jnp.float32
BF16 = jnp.bfloat16
F = 4096
NLAM = 20
BLK = 128
VD = 384
NB = 3
NS = 2
TEST = 1024
T = 768
Q = 1024
W = NS * BLK
NX = NY = NZ = 4
NC = 2
SMEM = pl.BlockSpec(memory_space=pltpu.SMEM)
VMEM = pl.BlockSpec(memory_space=pltpu.VMEM)
HBM = pl.BlockSpec(memory_space=pltpu.HBM)


def moves(target):
    pairs = []
    for x in range(NX):
        for y in range(NY):
            for z in range(NZ):
                for c in range(NC):
                    tx, ty, tz, tc = target(x, y, z, c)
                    source = ((x * NY + y) * NZ + z) * NC + c
                    goal = (((tx % NX) * NY + ty % NY) * NZ + tz % NZ) * NC + tc % NC
                    pairs.append((source, goal))
    return pairs


PRIMARY = moves(lambda x, y, z, c: (x + 1 - 2 * c, y, z, c))
SECONDARY = moves(lambda x, y, z, c: (x - 1 + 2 * c, y, z, c))
OPPOSITE = moves(lambda x, y, z, c: (x + 2, y, z, c))
SWAP = moves(lambda x, y, z, c: (x, y, z, c + 1))
FIRST = [moves(lambda x, y, z, c, d=d: (x, y + d * (1 - c), z + d * c, c)) for d in (1, 2, 3)]
UP = moves(lambda x, y, z, c: (x, y + c, z + 1 - c, c))
DOWN = moves(lambda x, y, z, c: (x, y - c, z - 1 + c, c))


def pin(*arrays):
    return [pltpu.with_memory_space_constraint(a, pltpu.HBM) for a in arrays]


def send(value, pairs):
    return lax.ppermute(value, ("tm", "vox"), pairs)


def place():
    x = lax.axis_index("tm")
    v = lax.axis_index("vox")
    return x, v // (NZ * NC), (v // NC) % NZ, v % NC


def slots(live):
    first = jnp.where(live[0] > 0, 0, jnp.where(live[1] > 0, 1, 2))
    second = jnp.where(live[2] > 0, 2, jnp.where(live[1] > 0, 1, 0))
    return first, second


def quarter(which, x, c):
    step = 1 - 2 * c
    if which == "primary":
        return (x + step + NX) % NX
    if which == "secondary":
        return (x - step + NX) % NX
    if which == "opposite":
        return (x + 2) % NX
    return x


SMALL = [
    pltpu.SMEM((NLAM,), F32),
    pltpu.SMEM((NB,), jnp.int32),
    pltpu.SMEM((NB,), jnp.int32),
    pltpu.VMEM((1, F), F32),
]


def scaled(total, q, picked, lambdas, lam_index, live, sing):
    s = sing[:, pl.ds(pl.multiple_of(q * Q, Q), Q)]
    parts = []
    for j, slot in enumerate(picked):
        scale = s / (s * s + lambdas[lam_index[slot]]) * live[slot].astype(F32)
        parts.append(total[j * BLK : (j + 1) * BLK, :] * scale)
    return parts


def start_kernel(lambdas_h, lam_index_h, live_h, sing_h, u, y, *rest):
    out, yt_out, lambdas, lam_index, live, sing, ys, us, sems = rest
    x, _, _, c = place()
    q = quarter("opposite", x, c)
    held = (lambdas, lam_index, live, sing)
    copies = [
        pltpu.make_async_copy(r, h, sems.at[i])
        for i, (r, h) in enumerate(zip((lambdas_h, lam_index_h, live_h, sing_h), held))
    ]
    for copy in copies:
        copy.start()
    wide = pltpu.make_async_copy(u.at[:, pl.ds(pl.multiple_of(q * Q, Q), Q)], us, sems.at[4])
    whole = pltpu.make_async_copy(y, ys, sems.at[5])
    whole.start()
    wide.start()
    for copy in copies:
        copy.wait()
    picked = slots(live)
    whole.wait()
    for j, slot in enumerate(picked):
        block = ys[:, pl.ds(pl.multiple_of(slot * BLK, BLK), BLK)]
        yt_out[j * BLK : (j + 1) * BLK, :] = block.T
    wide.wait()
    total = jnp.dot(yt_out[...], us[...], preferred_element_type=F32)
    for j, part in enumerate(scaled(total, q, picked, *held)):
        out[j * BLK : (j + 1) * BLK, :] = part.astype(out.dtype)


def start_call(lambdas, lam_index, live, sing, u, y):
    return pl.pallas_call(
        start_kernel,
        out_shape=[jax.ShapeDtypeStruct((W, Q), BF16), jax.ShapeDtypeStruct((W, T), BF16)],
        in_specs=[HBM] * 6,
        out_specs=[VMEM] * 2,
        scratch_shapes=SMALL
        + [pltpu.VMEM((T, VD), BF16), pltpu.VMEM((T, Q), BF16), pltpu.SemaphoreType.DMA((6,))],
        compiler_params=pltpu.CompilerParams(vmem_limit_bytes=8 << 20),
        cost_estimate=pl.CostEstimate(
            flops=2 * W * T * Q, bytes_accessed=2 * T * Q, transcendentals=0
        ),
    )(*pin(lambdas, lam_index, live, sing, u, y))


def rest_kernel(lambdas_h, lam_index_h, live_h, sing_h, u, yt, *rest):
    outs, (lambdas, lam_index, live, sing, us, sems) = rest[:3], rest[3:]
    x, _, _, c = place()
    where = [quarter(name, x, c) for name in ("primary", "secondary", "own")]
    held = (lambdas, lam_index, live, sing)
    copies = [
        pltpu.make_async_copy(r, h, sems.at[i])
        for i, (r, h) in enumerate(zip((lambdas_h, lam_index_h, live_h, sing_h), held))
    ]
    wide = [
        pltpu.make_async_copy(u.at[:, pl.ds(pl.multiple_of(q * Q, Q), Q)], us.at[i], sems.at[4 + i])
        for i, q in enumerate(where)
    ]
    for copy in copies + wide:
        copy.start()
    for copy in copies:
        copy.wait()
    picked = slots(live)
    for i, q in enumerate(where):
        wide[i].wait()
        total = jnp.dot(yt[...], us[i], preferred_element_type=F32)
        for j, part in enumerate(scaled(total, q, picked, *held)):
            outs[i][j * BLK : (j + 1) * BLK, :] = part.astype(outs[i].dtype)


def rest_call(lambdas, lam_index, live, sing, u, yt):
    return pl.pallas_call(
        rest_kernel,
        out_shape=[jax.ShapeDtypeStruct((W, Q), d) for d in (F32, BF16, F32)],
        in_specs=[HBM] * 5 + [VMEM],
        out_specs=[VMEM] * 3,
        scratch_shapes=SMALL + [pltpu.VMEM((3, T, Q), BF16), pltpu.SemaphoreType.DMA((7,))],
        compiler_params=pltpu.CompilerParams(vmem_limit_bytes=12 << 20),
        cost_estimate=pl.CostEstimate(
            flops=6 * W * T * Q, bytes_accessed=6 * T * Q, transcendentals=0
        ),
    )(*pin(lambdas, lam_index, live, sing, u), yt)


CHUNK = 256


def multiply(q, rows, shards, features):
    _, y, z0, c = place()
    back = (y - q + NY) % NY
    total = None
    for z in range(NZ):
        deep = (z0 - z + NZ) % NZ
        first = c * NY * NZ + deep * NY + back
        second = (1 - c) * NY * NZ + back * NZ + deep
        left = jnp.concatenate([shards[first, rows, :], shards[second, rows, :]], axis=1)
        right = features[:, z * NC * BLK : (z + 1) * NC * BLK]
        part = lax.dot_general(left, right, (((1,), (1,)), ((), ())), preferred_element_type=F32)
        total = part if total is None else total + part
    return total


def three_kernel(shards, own, primary, secondary, out):
    x, _, _, c = place()
    features = (own, primary, secondary)
    for r in range(Q // CHUNK):
        rows = slice(r * CHUNK, (r + 1) * CHUNK)
        total = None
        for i, name in enumerate(("own", "primary", "secondary")):
            part = multiply(quarter(name, x, c), rows, shards, features[i])
            total = part if total is None else total + part
        out[rows, :] = total


def three_call(shards, features):
    return pl.pallas_call(
        three_kernel,
        out_shape=jax.ShapeDtypeStruct((Q, W), F32),
        in_specs=[VMEM] * 4,
        out_specs=VMEM,
        compiler_params=pltpu.CompilerParams(vmem_limit_bytes=8 << 20),
        cost_estimate=pl.CostEstimate(
            flops=2 * W * 3 * Q * Q, bytes_accessed=2 * Q * 3 * Q, transcendentals=0
        ),
    )(shards, *features)


def spread(out, rows, values, live):
    first, second = slots(live)
    left, right = values[:, :BLK], values[:, BLK:]
    for b in range(NB):
        block = jnp.where(first == b, left, right)
        block = jnp.where(live[b] > 0, block, jnp.zeros_like(block))
        out[rows, b * BLK : (b + 1) * BLK] = block.astype(out.dtype)


def last_kernel(live_h, shards, features, so_far, tests, *rest):
    weights, mine, primary, secondary, opposite, live, packed, sem = rest
    copy = pltpu.make_async_copy(live_h, live, sem)
    copy.start()
    x, _, _, c = place()
    q = quarter("opposite", x, c)
    copy.wait()
    for r in range(Q // CHUNK):
        rows = slice(r * CHUNK, (r + 1) * CHUNK)
        total = (so_far[rows, :] + multiply(q, rows, shards, features)).astype(BF16)
        packed[rows, :] = total
        spread(weights, rows, total, live)
    count = TEST // NX
    for name, out in (
        ("opposite", opposite),
        ("primary", primary),
        ("secondary", secondary),
        ("own", mine),
    ):
        q = quarter(name, x, c)
        part = tests[pl.ds(pl.multiple_of(q * count, count), count), :]
        out[...] = jnp.dot(part, packed[...], preferred_element_type=F32).astype(out.dtype)


def last_call(live, shards, features, so_far, tests):
    rows = TEST // NX
    return pl.pallas_call(
        last_kernel,
        out_shape=[
            jax.ShapeDtypeStruct((Q, VD), BF16),
            jax.ShapeDtypeStruct((rows, W), F32),
            jax.ShapeDtypeStruct((rows, W), BF16),
            jax.ShapeDtypeStruct((rows, W), BF16),
            jax.ShapeDtypeStruct((rows, W), BF16),
        ],
        in_specs=[HBM] + [VMEM] * 4,
        out_specs=[VMEM] * 5,
        scratch_shapes=[
            pltpu.SMEM((NB,), jnp.int32),
            pltpu.VMEM((Q, W), BF16),
            pltpu.SemaphoreType.DMA,
        ],
        compiler_params=pltpu.CompilerParams(vmem_limit_bytes=8 << 20),
        cost_estimate=pl.CostEstimate(
            flops=4 * W * Q * Q, bytes_accessed=4 * Q * Q, transcendentals=0
        ),
    )(*pin(live), shards, features, so_far, tests)


def end_kernel(live_h, mine, a, b, c, out, live, sem):
    copy = pltpu.make_async_copy(live_h, live, sem)
    copy.start()
    total = mine[...] + a[...].astype(F32) + b[...].astype(F32) + c[...].astype(F32)
    copy.wait()
    spread(out, slice(0, TEST // NX), total, live)


def end_call(live, mine, a, b, c):
    return pl.pallas_call(
        end_kernel,
        out_shape=jax.ShapeDtypeStruct((TEST // NX, VD), BF16),
        in_specs=[HBM] + [VMEM] * 4,
        out_specs=VMEM,
        scratch_shapes=[pltpu.SMEM((NB,), jnp.int32), pltpu.SemaphoreType.DMA],
        compiler_params=pltpu.CompilerParams(vmem_limit_bytes=4 << 20),
    )(*pin(live), mine, a, b, c)


def body(u_train, y_train, sing, lambdas, lam_index, live, v_basis, x_test):
    sing = sing.reshape(1, F)
    small = (lambdas, lam_index, live, sing)
    p_opposite, yt = start_call(*small, u_train, y_train)
    come = send(p_opposite, PRIMARY)
    v_basis, yt = lax.optimization_barrier((v_basis, yt))
    near = [send(v_basis, pairs) for pairs in FIRST]
    p_primary, p_secondary, p_own = rest_call(*small, u_train, yt)
    row = jnp.stack([v_basis, *near])
    below = send(row, UP)
    above = send(row, DOWN)
    far_a = send(below[:2], UP)
    far_b = send(above[2:], DOWN)
    own = [row, below, far_a, far_b, above]
    other = [send(block, SWAP) for block in own]
    shards = jnp.concatenate(own + other)
    onward = (p_primary + come.astype(F32)).astype(BF16)
    from_secondary = send(onward, PRIMARY)
    from_primary = send(p_secondary, SECONDARY)
    filtered = (p_own + from_secondary.astype(F32) + from_primary.astype(F32)).astype(BF16)
    f_secondary = send(filtered, PRIMARY)
    f_primary = send(filtered, SECONDARY)
    f_opposite = send(f_secondary, PRIMARY)
    so_far = three_call(shards, (filtered, f_primary, f_secondary))
    weights, mine, primary, secondary, opposite = last_call(
        live, shards, f_opposite, so_far, x_test
    )
    predictions = end_call(
        live, mine, send(opposite, OPPOSITE), send(primary, PRIMARY), send(secondary, SECONDARY)
    )
    return weights, predictions


def solution(mesh):
    placed = (
        P("tm", None),
        P("tm", "vox"),
        P(),
        P(),
        P("vox"),
        P("vox"),
        P("tm", "vox"),
        P(None, "tm"),
    )
    return jax.shard_map(
        body,
        mesh=mesh,
        in_specs=placed,
        out_specs=(P("tm", "vox"), P("tm", "vox")),
        check_vma=False,
    )
```

```python
import functools

import jax
import jax.numpy as jnp
from jax import lax
from jax.experimental import pallas as pl
from jax.experimental.pallas import tpu as pltpu
from jax.sharding import PartitionSpec as P

F32 = jnp.float32
BF16 = jnp.bfloat16
F = 4096
NLAM = 20
BLK = 128
VD = 384
NB = 3
NS = 2
TEST = 1024
T = 768
Q = 1024
W = NS * BLK
NX = NY = NZ = 4
NC = 2
SMEM = pl.BlockSpec(memory_space=pltpu.SMEM)
VMEM = pl.BlockSpec(memory_space=pltpu.VMEM)
HBM = pl.BlockSpec(memory_space=pltpu.HBM)


def moves(target):
    pairs = []
    for x in range(NX):
        for y in range(NY):
            for z in range(NZ):
                for c in range(NC):
                    tx, ty, tz, tc = target(x, y, z, c)
                    source = ((x * NY + y) * NZ + z) * NC + c
                    goal = (((tx % NX) * NY + ty % NY) * NZ + tz % NZ) * NC + tc % NC
                    pairs.append((source, goal))
    return pairs


PRIMARY = moves(lambda x, y, z, c: (x + 1 - 2 * c, y, z, c))
SECONDARY = moves(lambda x, y, z, c: (x - 1 + 2 * c, y, z, c))
OPPOSITE = moves(lambda x, y, z, c: (x + 2, y, z, c))
SWAP = moves(lambda x, y, z, c: (x, y, z, c + 1))
FIRST = [moves(lambda x, y, z, c, d=d: (x, y + d * (1 - c), z + d * c, c)) for d in (1, 2, 3)]
UP = moves(lambda x, y, z, c: (x, y + c, z + 1 - c, c))
DOWN = moves(lambda x, y, z, c: (x, y - c, z - 1 + c, c))


def pin(*arrays):
    return [pltpu.with_memory_space_constraint(a, pltpu.HBM) for a in arrays]


def send(value, pairs):
    return lax.ppermute(value, ("tm", "vox"), pairs)


def place():
    x = lax.axis_index("tm")
    v = lax.axis_index("vox")
    return x, v // (NZ * NC), (v // NC) % NZ, v % NC


def slots(live):
    first = jnp.where(live[0] > 0, 0, jnp.where(live[1] > 0, 1, 2))
    second = jnp.where(live[2] > 0, 2, jnp.where(live[1] > 0, 1, 0))
    return first, second


def quarter(which, x, c):
    step = 1 - 2 * c
    if which == "primary":
        return (x + step + NX) % NX
    if which == "secondary":
        return (x - step + NX) % NX
    if which == "opposite":
        return (x + 2) % NX
    return x


SMALL = [
    pltpu.SMEM((NLAM,), F32),
    pltpu.SMEM((NB,), jnp.int32),
    pltpu.SMEM((NB,), jnp.int32),
    pltpu.VMEM((1, F), F32),
]


def scaled(total, q, picked, lambdas, lam_index, live, sing):
    s = sing[:, pl.ds(pl.multiple_of(q * Q, Q), Q)]
    parts = []
    for j, slot in enumerate(picked):
        scale = s / (s * s + lambdas[lam_index[slot]]) * live[slot].astype(F32)
        parts.append(total[j * BLK : (j + 1) * BLK, :] * scale)
    return parts


def start_kernel(lambdas_h, lam_index_h, live_h, sing_h, u, y, *rest):
    out, yt_out, lambdas, lam_index, live, sing, ys, us, sems = rest
    x, _, _, c = place()
    q = quarter("opposite", x, c)
    held = (lambdas, lam_index, live, sing)
    copies = [
        pltpu.make_async_copy(r, h, sems.at[i])
        for i, (r, h) in enumerate(zip((lambdas_h, lam_index_h, live_h, sing_h), held))
    ]
    for copy in copies:
        copy.start()
    wide = pltpu.make_async_copy(u.at[:, pl.ds(pl.multiple_of(q * Q, Q), Q)], us, sems.at[4])
    whole = pltpu.make_async_copy(y, ys, sems.at[5])
    whole.start()
    wide.start()
    for copy in copies:
        copy.wait()
    picked = slots(live)
    whole.wait()
    for j, slot in enumerate(picked):
        block = ys[:, pl.ds(pl.multiple_of(slot * BLK, BLK), BLK)]
        yt_out[j * BLK : (j + 1) * BLK, :] = block.T
    wide.wait()
    total = jnp.dot(yt_out[...], us[...], preferred_element_type=F32)
    for j, part in enumerate(scaled(total, q, picked, *held)):
        out[j * BLK : (j + 1) * BLK, :] = part.astype(out.dtype)


def start_call(lambdas, lam_index, live, sing, u, y):
    return pl.pallas_call(
        start_kernel,
        out_shape=[jax.ShapeDtypeStruct((W, Q), BF16), jax.ShapeDtypeStruct((W, T), BF16)],
        in_specs=[HBM] * 6,
        out_specs=[VMEM] * 2,
        scratch_shapes=SMALL
        + [pltpu.VMEM((T, VD), BF16), pltpu.VMEM((T, Q), BF16), pltpu.SemaphoreType.DMA((6,))],
        compiler_params=pltpu.CompilerParams(vmem_limit_bytes=8 << 20),
        cost_estimate=pl.CostEstimate(
            flops=2 * W * T * Q, bytes_accessed=2 * T * Q, transcendentals=0
        ),
    )(*pin(lambdas, lam_index, live, sing, u, y))


def rest_kernel(lambdas_h, lam_index_h, live_h, sing_h, u, yt, *rest):
    outs, (lambdas, lam_index, live, sing, us, sems) = rest[:3], rest[3:]
    x, _, _, c = place()
    where = [quarter(name, x, c) for name in ("primary", "secondary", "own")]
    held = (lambdas, lam_index, live, sing)
    copies = [
        pltpu.make_async_copy(r, h, sems.at[i])
        for i, (r, h) in enumerate(zip((lambdas_h, lam_index_h, live_h, sing_h), held))
    ]
    wide = [
        pltpu.make_async_copy(u.at[:, pl.ds(pl.multiple_of(q * Q, Q), Q)], us.at[i], sems.at[4 + i])
        for i, q in enumerate(where)
    ]
    for copy in copies + wide:
        copy.start()
    for copy in copies:
        copy.wait()
    picked = slots(live)
    for i, q in enumerate(where):
        wide[i].wait()
        total = jnp.dot(yt[...], us[i], preferred_element_type=F32)
        for j, part in enumerate(scaled(total, q, picked, *held)):
            outs[i][j * BLK : (j + 1) * BLK, :] = part.astype(outs[i].dtype)


def rest_call(lambdas, lam_index, live, sing, u, yt):
    return pl.pallas_call(
        rest_kernel,
        out_shape=[jax.ShapeDtypeStruct((W, Q), d) for d in (F32, BF16, F32)],
        in_specs=[HBM] * 5 + [VMEM],
        out_specs=[VMEM] * 3,
        scratch_shapes=SMALL + [pltpu.VMEM((3, T, Q), BF16), pltpu.SemaphoreType.DMA((7,))],
        compiler_params=pltpu.CompilerParams(vmem_limit_bytes=12 << 20),
        cost_estimate=pl.CostEstimate(
            flops=6 * W * T * Q, bytes_accessed=6 * T * Q, transcendentals=0
        ),
    )(*pin(lambdas, lam_index, live, sing, u), yt)


CHUNK = 256


def block_of(distance):
    return jnp.where(distance == 3, 2, jnp.where(distance == 2, 3, distance))


def multiply(q, rows, shards, features):
    _, y, z0, c = place()
    back = (y - q + NY) % NY
    total = None
    for z in range(NZ):
        deep = (z0 - z + NZ) % NZ
        first = c * NY * NZ + block_of(deep) * NY + back
        second = (1 - c) * NY * NZ + block_of(back) * NZ + deep
        left = jnp.concatenate([shards[first, rows, :], shards[second, rows, :]], axis=1)
        right = features[:, z * NC * BLK : (z + 1) * NC * BLK]
        part = lax.dot_general(left, right, (((1,), (1,)), ((), ())), preferred_element_type=F32)
        total = part if total is None else total + part
    return total


def three_kernel(shards, own, primary, secondary, out):
    x, _, _, c = place()
    features = (own, primary, secondary)
    for r in range(Q // CHUNK):
        rows = slice(r * CHUNK, (r + 1) * CHUNK)
        total = None
        for i, name in enumerate(("own", "primary", "secondary")):
            part = multiply(quarter(name, x, c), rows, shards, features[i])
            total = part if total is None else total + part
        out[rows, :] = total


def three_call(shards, features):
    return pl.pallas_call(
        three_kernel,
        out_shape=jax.ShapeDtypeStruct((Q, W), F32),
        in_specs=[VMEM] * 4,
        out_specs=VMEM,
        compiler_params=pltpu.CompilerParams(vmem_limit_bytes=8 << 20),
        cost_estimate=pl.CostEstimate(
            flops=2 * W * 3 * Q * Q, bytes_accessed=2 * Q * 3 * Q, transcendentals=0
        ),
    )(shards, *features)


def spread(out, rows, values, live):
    first, second = slots(live)
    left, right = values[:, :BLK], values[:, BLK:]
    for b in range(NB):
        block = jnp.where(first == b, left, right)
        block = jnp.where(live[b] > 0, block, jnp.zeros_like(block))
        out[rows, b * BLK : (b + 1) * BLK] = block.astype(out.dtype)


def last_kernel(live_h, shards, features, so_far, tests, *rest):
    weights, mine, primary, secondary, opposite, live, packed, sem = rest
    copy = pltpu.make_async_copy(live_h, live, sem)
    copy.start()
    x, _, _, c = place()
    q = quarter("opposite", x, c)
    copy.wait()
    for r in range(Q // CHUNK):
        rows = slice(r * CHUNK, (r + 1) * CHUNK)
        total = (so_far[rows, :] + multiply(q, rows, shards, features)).astype(BF16)
        packed[rows, :] = total
        spread(weights, rows, total, live)
    count = TEST // NX
    for name, out in (
        ("opposite", opposite),
        ("primary", primary),
        ("secondary", secondary),
        ("own", mine),
    ):
        q = quarter(name, x, c)
        part = tests[pl.ds(pl.multiple_of(q * count, count), count), :]
        out[...] = jnp.dot(part, packed[...], preferred_element_type=F32).astype(out.dtype)


def last_call(live, shards, features, so_far, tests):
    rows = TEST // NX
    return pl.pallas_call(
        last_kernel,
        out_shape=[
            jax.ShapeDtypeStruct((Q, VD), BF16),
            jax.ShapeDtypeStruct((rows, W), F32),
            jax.ShapeDtypeStruct((rows, W), BF16),
            jax.ShapeDtypeStruct((rows, W), BF16),
            jax.ShapeDtypeStruct((rows, W), BF16),
        ],
        in_specs=[HBM] + [VMEM] * 4,
        out_specs=[VMEM] * 5,
        scratch_shapes=[
            pltpu.SMEM((NB,), jnp.int32),
            pltpu.VMEM((Q, W), BF16),
            pltpu.SemaphoreType.DMA,
        ],
        compiler_params=pltpu.CompilerParams(vmem_limit_bytes=8 << 20),
        cost_estimate=pl.CostEstimate(
            flops=4 * W * Q * Q, bytes_accessed=4 * Q * Q, transcendentals=0
        ),
    )(*pin(live), shards, features, so_far, tests)


def end_kernel(live_h, mine, a, b, c, out, live, sem):
    copy = pltpu.make_async_copy(live_h, live, sem)
    copy.start()
    total = mine[...] + a[...].astype(F32) + b[...].astype(F32) + c[...].astype(F32)
    copy.wait()
    spread(out, slice(0, TEST // NX), total, live)


def end_call(live, mine, a, b, c):
    return pl.pallas_call(
        end_kernel,
        out_shape=jax.ShapeDtypeStruct((TEST // NX, VD), BF16),
        in_specs=[HBM] + [VMEM] * 4,
        out_specs=VMEM,
        scratch_shapes=[pltpu.SMEM((NB,), jnp.int32), pltpu.SemaphoreType.DMA],
        compiler_params=pltpu.CompilerParams(vmem_limit_bytes=4 << 20),
    )(*pin(live), mine, a, b, c)


def body(u_train, y_train, sing, lambdas, lam_index, live, v_basis, x_test):
    sing = sing.reshape(1, F)
    small = (lambdas, lam_index, live, sing)
    p_opposite, yt = start_call(*small, u_train, y_train)
    come = send(p_opposite, PRIMARY)
    p_primary, p_secondary, p_own = rest_call(*small, u_train, yt)
    v_basis, _ = lax.optimization_barrier((v_basis, yt))
    near = [send(v_basis, pairs) for pairs in FIRST]
    row = jnp.stack([v_basis, *near])
    below = send(row, UP)
    above = send(row, DOWN)
    onward = (p_primary + come.astype(F32)).astype(BF16)
    from_secondary = send(onward, PRIMARY)
    from_primary = send(p_secondary, SECONDARY)
    filtered = (p_own + from_secondary.astype(F32) + from_primary.astype(F32)).astype(BF16)
    f_secondary = send(filtered, PRIMARY)
    f_primary = send(filtered, SECONDARY)
    below, above, _ = lax.optimization_barrier((below, above, filtered))
    far_a = send(below[:2], UP)
    far_b = send(above[2:], DOWN)
    early = jnp.concatenate([row, below, above])
    early_other = send(early, SWAP)
    f_secondary, f_primary, far_a, far_b = lax.optimization_barrier(
        (f_secondary, f_primary, far_a, far_b)
    )
    f_opposite = send(f_secondary, PRIMARY)
    late = jnp.concatenate([far_a, far_b])
    late_other = send(late, SWAP)
    shards = jnp.concatenate([early, late, early_other, late_other])
    so_far = three_call(shards, (filtered, f_primary, f_secondary))
    weights, mine, primary, secondary, opposite = last_call(
        live, shards, f_opposite, so_far, x_test
    )
    predictions = end_call(
        live, mine, send(opposite, OPPOSITE), send(primary, PRIMARY), send(secondary, SECONDARY)
    )
    return weights, predictions


def solution(mesh):
    placed = (
        P("tm", None),
        P("tm", "vox"),
        P(),
        P(),
        P("vox"),
        P("vox"),
        P("tm", "vox"),
        P(None, "tm"),
    )
    return jax.shard_map(
        body,
        mesh=mesh,
        in_specs=placed,
        out_specs=(P("tm", "vox"), P("tm", "vox")),
        check_vma=False,
    )
```

```python
import functools

import jax
import jax.numpy as jnp
from jax import lax
from jax.experimental import pallas as pl
from jax.experimental.pallas import tpu as pltpu
from jax.sharding import PartitionSpec as P

F32 = jnp.float32
BF16 = jnp.bfloat16
F = 4096
NLAM = 20
BLK = 128
VD = 384
NB = 3
NS = 2
TEST = 1024
T = 768
Q = 1024
W = NS * BLK
ROW_COST = 10_000_000_000
PASS_COST = 50_000_000_000
NX = NY = NZ = 4
NC = 2
SMEM = pl.BlockSpec(memory_space=pltpu.SMEM)
VMEM = pl.BlockSpec(memory_space=pltpu.VMEM)
HBM = pl.BlockSpec(memory_space=pltpu.HBM)


def moves(target):
    pairs = []
    for x in range(NX):
        for y in range(NY):
            for z in range(NZ):
                for c in range(NC):
                    tx, ty, tz, tc = target(x, y, z, c)
                    source = ((x * NY + y) * NZ + z) * NC + c
                    goal = (((tx % NX) * NY + ty % NY) * NZ + tz % NZ) * NC + tc % NC
                    pairs.append((source, goal))
    return pairs


PAIR_A = moves(lambda x, y, z, c: (3 - x if c else x ^ 1, y, z, c))
PAIR_B = moves(lambda x, y, z, c: (x ^ 1 if c else 3 - x, y, z, c))
OPPOSITE = moves(lambda x, y, z, c: (x + 2, y, z, c))
SWAP = moves(lambda x, y, z, c: (x, y, z, c + 1))
FIRST = [moves(lambda x, y, z, c, d=d: (x, y + d * (1 - c), z + d * c, c)) for d in (1, 2, 3)]
UP = moves(lambda x, y, z, c: (x, y + c, z + 1 - c, c))
DOWN = moves(lambda x, y, z, c: (x, y - c, z - 1 + c, c))


def pin(*arrays):
    return [pltpu.with_memory_space_constraint(a, pltpu.HBM) for a in arrays]


def send(value, pairs):
    return lax.ppermute(value, ("tm", "vox"), pairs)


def place():
    x = lax.axis_index("tm")
    v = lax.axis_index("vox")
    return x, v // (NZ * NC), (v // NC) % NZ, v % NC


def slots(live):
    first = jnp.where(live[0] > 0, 0, jnp.where(live[1] > 0, 1, 2))
    second = jnp.where(live[2] > 0, 2, jnp.where(live[1] > 0, 1, 0))
    return first, second


def quarter(which, x, c):
    flipped = x + 1 - 2 * (x % 2)
    mirrored = NX - 1 - x
    if which == "a":
        return jnp.where(c == 0, flipped, mirrored)
    if which == "b":
        return jnp.where(c == 0, mirrored, flipped)
    if which == "opposite":
        return (x + 2) % NX
    return x


SMALL = [
    pltpu.SMEM((NLAM,), F32),
    pltpu.SMEM((NB,), jnp.int32),
    pltpu.SMEM((NB,), jnp.int32),
    pltpu.VMEM((1, F), F32),
]


def scaled(total, q, picked, lambdas, lam_index, live, sing):
    s = sing[:, pl.ds(pl.multiple_of(q * Q, Q), Q)]
    parts = []
    for j, slot in enumerate(picked):
        scale = s / (s * s + lambdas[lam_index[slot]]) * live[slot].astype(F32)
        parts.append(total[j * BLK : (j + 1) * BLK, :] * scale)
    return parts


def products(where, outs, yt, us, wide, picked, held):
    for i, q in enumerate(where):
        wide[i].wait()
        total = jnp.dot(yt[...], us[i], preferred_element_type=F32)
        for j, part in enumerate(scaled(total, q, picked, *held)):
            outs[i][j * BLK : (j + 1) * BLK, :] = part.astype(outs[i].dtype)


def start_kernel(lambdas_h, lam_index_h, live_h, sing_h, u, y, *rest):
    out, yt_out, lambdas, lam_index, live, sing, ys, us, sems = rest
    x, _, _, c = place()
    where = [quarter(name, x, c) for name in ("a", "opposite")]
    held = (lambdas, lam_index, live, sing)
    copies = [
        pltpu.make_async_copy(r, h, sems.at[i])
        for i, (r, h) in enumerate(zip((lambdas_h, lam_index_h, live_h, sing_h), held))
    ]
    whole = pltpu.make_async_copy(y, ys, sems.at[4])
    wide = [
        pltpu.make_async_copy(u.at[:, pl.ds(pl.multiple_of(q * Q, Q), Q)], us.at[i], sems.at[5 + i])
        for i, q in enumerate(where)
    ]
    for copy in copies + [whole] + wide:
        copy.start()
    for copy in copies:
        copy.wait()
    picked = slots(live)
    whole.wait()
    for j, slot in enumerate(picked):
        block = ys[:, pl.ds(pl.multiple_of(slot * BLK, BLK), BLK)]
        yt_out[j * BLK : (j + 1) * BLK, :] = block.T
    products(where, [out.at[0], out.at[1]], yt_out, us, wide, picked, held)


def start_call(lambdas, lam_index, live, sing, u, y):
    return pl.pallas_call(
        start_kernel,
        out_shape=[jax.ShapeDtypeStruct((2, W, Q), BF16), jax.ShapeDtypeStruct((W, T), BF16)],
        in_specs=[HBM] * 6,
        out_specs=[VMEM] * 2,
        scratch_shapes=SMALL
        + [pltpu.VMEM((T, VD), BF16), pltpu.VMEM((2, T, Q), BF16), pltpu.SemaphoreType.DMA((7,))],
        compiler_params=pltpu.CompilerParams(vmem_limit_bytes=10 << 20),
        cost_estimate=pl.CostEstimate(
            flops=4 * W * T * Q, bytes_accessed=4 * T * Q, transcendentals=0
        ),
    )(*pin(lambdas, lam_index, live, sing, u, y))


def rest_kernel(lambdas_h, lam_index_h, live_h, sing_h, u, yt, *rest):
    outs, (lambdas, lam_index, live, sing, us, sems) = rest[:2], rest[2:]
    x, _, _, c = place()
    where = [quarter(name, x, c) for name in ("b", "own")]
    held = (lambdas, lam_index, live, sing)
    copies = [
        pltpu.make_async_copy(r, h, sems.at[i])
        for i, (r, h) in enumerate(zip((lambdas_h, lam_index_h, live_h, sing_h), held))
    ]
    wide = [
        pltpu.make_async_copy(u.at[:, pl.ds(pl.multiple_of(q * Q, Q), Q)], us.at[i], sems.at[4 + i])
        for i, q in enumerate(where)
    ]
    for copy in copies + wide:
        copy.start()
    for copy in copies:
        copy.wait()
    products(where, outs, yt, us, wide, slots(live), held)


def rest_call(lambdas, lam_index, live, sing, u, yt):
    return pl.pallas_call(
        rest_kernel,
        out_shape=[jax.ShapeDtypeStruct((W, Q), F32)] * 2,
        in_specs=[HBM] * 5 + [VMEM],
        out_specs=[VMEM] * 2,
        scratch_shapes=SMALL + [pltpu.VMEM((2, T, Q), BF16), pltpu.SemaphoreType.DMA((6,))],
        compiler_params=pltpu.CompilerParams(vmem_limit_bytes=10 << 20),
        cost_estimate=pl.CostEstimate(
            flops=4 * W * T * Q, bytes_accessed=4 * T * Q, transcendentals=0
        ),
    )(*pin(lambdas, lam_index, live, sing, u), yt)


def row_kernel(a, b, c, d, out):
    for i, block in enumerate((a, b, c, d)):
        out[i] = block[...]


def row_call(*blocks):
    return pl.pallas_call(
        row_kernel,
        out_shape=jax.ShapeDtypeStruct((NY, Q, BLK), BF16),
        in_specs=[VMEM] * 4,
        out_specs=VMEM,
        compiler_params=pltpu.CompilerParams(vmem_limit_bytes=2 << 20),
        cost_estimate=pl.CostEstimate(
            flops=ROW_COST, bytes_accessed=4 * Q * Q, transcendentals=0
        ),
    )(*blocks)


def pass_kernel(value, out):
    pass


def pass_call(value):
    return pl.pallas_call(
        pass_kernel,
        out_shape=jax.ShapeDtypeStruct(value.shape, value.dtype),
        in_specs=[VMEM],
        out_specs=VMEM,
        input_output_aliases={0: 0},
        compiler_params=pltpu.CompilerParams(vmem_limit_bytes=1 << 20),
        cost_estimate=pl.CostEstimate(
            flops=PASS_COST, bytes_accessed=4 * Q * Q, transcendentals=0
        ),
    )(value)


CHUNK = 256


def block_of(distance):
    return jnp.where(distance == 3, 2, jnp.where(distance == 2, 3, distance))


def multiply(q, rows, shards, features):
    _, y, z0, c = place()
    back = (y - q + NY) % NY
    total = None
    for z in range(NZ):
        deep = (z0 - z + NZ) % NZ
        first = c * NY * NZ + block_of(deep) * NY + back
        second = (1 - c) * NY * NZ + block_of(back) * NZ + deep
        left = jnp.concatenate([shards[first, rows, :], shards[second, rows, :]], axis=1)
        right = features[:, z * NC * BLK : (z + 1) * NC * BLK]
        part = lax.dot_general(left, right, (((1,), (1,)), ((), ())), preferred_element_type=F32)
        total = part if total is None else total + part
    return total


def half_kernel(shards, own, other, out):
    x, _, _, c = place()
    for r in range(Q // CHUNK):
        rows = slice(r * CHUNK, (r + 1) * CHUNK)
        out[rows, :] = multiply(x, rows, shards, own) + multiply(
            quarter("b", x, c), rows, shards, other
        )


def half_call(shards, own, other):
    return pl.pallas_call(
        half_kernel,
        out_shape=jax.ShapeDtypeStruct((Q, W), F32),
        in_specs=[VMEM] * 3,
        out_specs=VMEM,
        compiler_params=pltpu.CompilerParams(vmem_limit_bytes=8 << 20),
        cost_estimate=pl.CostEstimate(
            flops=2 * W * 2 * Q * Q, bytes_accessed=2 * Q * 2 * Q, transcendentals=0
        ),
    )(shards, own, other)


def spread(out, rows, values, live):
    first, second = slots(live)
    left, right = values[:, :BLK], values[:, BLK:]
    for b in range(NB):
        block = jnp.where(first == b, left, right)
        block = jnp.where(live[b] > 0, block, jnp.zeros_like(block))
        out[rows, b * BLK : (b + 1) * BLK] = block.astype(out.dtype)


def last_kernel(live_h, shards, features, so_far, tests, *rest):
    weights, mine, to_a, to_b, opposite, live, packed, sem = rest
    copy = pltpu.make_async_copy(live_h, live, sem)
    copy.start()
    x, _, _, c = place()
    copy.wait()
    for r in range(Q // CHUNK):
        rows = slice(r * CHUNK, (r + 1) * CHUNK)
        total = so_far[rows, :]
        for i, name in enumerate(("a", "opposite")):
            total = total + multiply(quarter(name, x, c), rows, shards, features.at[i])
        total = total.astype(BF16)
        packed[rows, :] = total
        spread(weights, rows, total, live)
    count = TEST // NX
    for name, out in (
        ("opposite", opposite),
        ("a", to_a),
        ("b", to_b),
        ("own", mine),
    ):
        q = quarter(name, x, c)
        part = tests[pl.ds(pl.multiple_of(q * count, count), count), :]
        out[...] = jnp.dot(part, packed[...], preferred_element_type=F32).astype(out.dtype)


def last_call(live, shards, features, so_far, tests):
    rows = TEST // NX
    return pl.pallas_call(
        last_kernel,
        out_shape=[
            jax.ShapeDtypeStruct((Q, VD), BF16),
            jax.ShapeDtypeStruct((rows, W), F32),
            jax.ShapeDtypeStruct((rows, W), BF16),
            jax.ShapeDtypeStruct((rows, W), BF16),
            jax.ShapeDtypeStruct((rows, W), BF16),
        ],
        in_specs=[HBM] + [VMEM] * 4,
        out_specs=[VMEM] * 5,
        scratch_shapes=[
            pltpu.SMEM((NB,), jnp.int32),
            pltpu.VMEM((Q, W), BF16),
            pltpu.SemaphoreType.DMA,
        ],
        compiler_params=pltpu.CompilerParams(vmem_limit_bytes=8 << 20),
        cost_estimate=pl.CostEstimate(
            flops=4 * W * Q * Q, bytes_accessed=4 * Q * Q, transcendentals=0
        ),
    )(*pin(live), shards, features, so_far, tests)


def end_kernel(live_h, mine, a, b, c, out, live, sem):
    copy = pltpu.make_async_copy(live_h, live, sem)
    copy.start()
    total = mine[...] + a[...].astype(F32) + b[...].astype(F32) + c[...].astype(F32)
    copy.wait()
    spread(out, slice(0, TEST // NX), total, live)


def end_call(live, mine, a, b, c):
    return pl.pallas_call(
        end_kernel,
        out_shape=jax.ShapeDtypeStruct((TEST // NX, VD), BF16),
        in_specs=[HBM] + [VMEM] * 4,
        out_specs=VMEM,
        scratch_shapes=[pltpu.SMEM((NB,), jnp.int32), pltpu.SemaphoreType.DMA],
        compiler_params=pltpu.CompilerParams(vmem_limit_bytes=4 << 20),
    )(*pin(live), mine, a, b, c)


def body(u_train, y_train, sing, lambdas, lam_index, live, v_basis, x_test):
    sing = sing.reshape(1, F)
    small = (lambdas, lam_index, live, sing)
    p_send, yt = start_call(*small, u_train, y_train)
    come = send(p_send, PAIR_A)
    p_b, p_own = rest_call(*small, u_train, yt)
    near = [send(v_basis, pairs) for pairs in FIRST]
    row = row_call(v_basis, *near)
    below = send(row, UP)
    above = send(row, DOWN)
    from_b = send((p_b + come[1].astype(F32)).astype(BF16), PAIR_B)
    filtered = (p_own + come[0].astype(F32) + from_b.astype(F32)).astype(BF16)
    f_b = send(filtered, PAIR_B)
    below, above, f_b = lax.optimization_barrier((below, above, f_b))
    f_far = pass_call(send(jnp.stack([filtered, f_b]), PAIR_A))
    far_a = send(below[:2], UP)
    far_b = send(above[2:], DOWN)
    early = jnp.concatenate([row, below, above])
    early_other = send(early, SWAP)
    late = jnp.concatenate([far_a, far_b])
    late_other = send(late, SWAP)
    shards = jnp.concatenate([early, late, early_other, late_other])
    so_far = half_call(shards, filtered, f_b)
    weights, mine, to_a, to_b, opposite = last_call(live, shards, f_far, so_far, x_test)
    predictions = end_call(
        live, mine, send(opposite, OPPOSITE), send(to_a, PAIR_A), send(to_b, PAIR_B)
    )
    return weights, predictions


def solution(mesh):
    placed = (
        P("tm", None),
        P("tm", "vox"),
        P(),
        P(),
        P("vox"),
        P("vox"),
        P("tm", "vox"),
        P(None, "tm"),
    )
    return jax.shard_map(
        body,
        mesh=mesh,
        in_specs=placed,
        out_specs=(P("tm", "vox"), P("tm", "vox")),
        check_vma=False,
    )
```

```python
import functools

import jax
import jax.numpy as jnp
from jax import lax
from jax.experimental import pallas as pl
from jax.experimental.pallas import tpu as pltpu
from jax.sharding import PartitionSpec as P

F32 = jnp.float32
BF16 = jnp.bfloat16
F = 4096
NLAM = 20
BLK = 128
VD = 384
NB = 3
NS = 2
TEST = 1024
T = 768
Q = 1024
W = NS * BLK
ROW_COST = 10_000_000_000
PASS_COST = 50_000_000_000
LITTLE_COST = 500_000_000
NX = NY = NZ = 4
NC = 2
SMEM = pl.BlockSpec(memory_space=pltpu.SMEM)
VMEM = pl.BlockSpec(memory_space=pltpu.VMEM)
HBM = pl.BlockSpec(memory_space=pltpu.HBM)


def moves(target):
    pairs = []
    for x in range(NX):
        for y in range(NY):
            for z in range(NZ):
                for c in range(NC):
                    tx, ty, tz, tc = target(x, y, z, c)
                    source = ((x * NY + y) * NZ + z) * NC + c
                    goal = (((tx % NX) * NY + ty % NY) * NZ + tz % NZ) * NC + tc % NC
                    pairs.append((source, goal))
    return pairs


PAIR_A = moves(lambda x, y, z, c: (3 - x if c else x ^ 1, y, z, c))
PAIR_B = moves(lambda x, y, z, c: (x ^ 1 if c else 3 - x, y, z, c))
OPPOSITE = moves(lambda x, y, z, c: (x + 2, y, z, c))
SWAP = moves(lambda x, y, z, c: (x, y, z, c + 1))
FIRST = [moves(lambda x, y, z, c, d=d: (x, y + d * (1 - c), z + d * c, c)) for d in (1, 2, 3)]
UP = moves(lambda x, y, z, c: (x, y + c, z + 1 - c, c))
DOWN = moves(lambda x, y, z, c: (x, y - c, z - 1 + c, c))


def pin(*arrays):
    return [pltpu.with_memory_space_constraint(a, pltpu.HBM) for a in arrays]


def send(value, pairs):
    return lax.ppermute(value, ("tm", "vox"), pairs)


def after(value, other):
    return lax.optimization_barrier((value, other))[0]


def place():
    x = lax.axis_index("tm")
    v = lax.axis_index("vox")
    return x, v // (NZ * NC), (v // NC) % NZ, v % NC


def slots(live):
    first = jnp.where(live[0] > 0, 0, jnp.where(live[1] > 0, 1, 2))
    second = jnp.where(live[2] > 0, 2, jnp.where(live[1] > 0, 1, 0))
    return first, second


def quarter(which, x, c):
    flipped = x + 1 - 2 * (x % 2)
    mirrored = NX - 1 - x
    if which == "a":
        return jnp.where(c == 0, flipped, mirrored)
    if which == "b":
        return jnp.where(c == 0, mirrored, flipped)
    if which == "opposite":
        return (x + 2) % NX
    return x


SMALL = [
    pltpu.SMEM((NLAM,), F32),
    pltpu.SMEM((NB,), jnp.int32),
    pltpu.SMEM((NB,), jnp.int32),
    pltpu.VMEM((1, F), F32),
]


def scaled(total, q, picked, lambdas, lam_index, live, sing):
    s = sing[:, pl.ds(pl.multiple_of(q * Q, Q), Q)]
    parts = []
    for j, slot in enumerate(picked):
        scale = s / (s * s + lambdas[lam_index[slot]]) * live[slot].astype(F32)
        parts.append(total[j * BLK : (j + 1) * BLK, :] * scale)
    return parts


def products(where, outs, yt, us, wide, picked, held):
    for i, q in enumerate(where):
        wide[i].wait()
        total = jnp.dot(yt[...], us[i], preferred_element_type=F32)
        for j, part in enumerate(scaled(total, q, picked, *held)):
            outs[i][j][...] = part.astype(outs[i][j].dtype)


def start_kernel(lambdas_h, lam_index_h, live_h, sing_h, u, y, *rest):
    out_0, out_1, yt_out, lambdas, lam_index, live, sing, ys, us, sems = rest
    x, _, _, c = place()
    where = [quarter(name, x, c) for name in ("a", "opposite")]
    held = (lambdas, lam_index, live, sing)
    copies = [
        pltpu.make_async_copy(r, h, sems.at[i])
        for i, (r, h) in enumerate(zip((lambdas_h, lam_index_h, live_h, sing_h), held))
    ]
    whole = pltpu.make_async_copy(y, ys, sems.at[4])
    wide = [
        pltpu.make_async_copy(u.at[:, pl.ds(pl.multiple_of(q * Q, Q), Q)], us.at[i], sems.at[5 + i])
        for i, q in enumerate(where)
    ]
    for copy in copies + [whole] + wide:
        copy.start()
    for copy in copies:
        copy.wait()
    picked = slots(live)
    whole.wait()
    for j, slot in enumerate(picked):
        block = ys[:, pl.ds(pl.multiple_of(slot * BLK, BLK), BLK)]
        yt_out[j * BLK : (j + 1) * BLK, :] = block.T
    outs = [[out_0.at[i], out_1.at[i]] for i in range(2)]
    products(where, outs, yt_out, us, wide, picked, held)


def start_call(lambdas, lam_index, live, sing, u, y):
    return pl.pallas_call(
        start_kernel,
        out_shape=[jax.ShapeDtypeStruct((2, BLK, Q), BF16)] * 2
        + [jax.ShapeDtypeStruct((W, T), BF16)],
        in_specs=[HBM] * 6,
        out_specs=[VMEM] * 3,
        scratch_shapes=SMALL
        + [pltpu.VMEM((T, VD), BF16), pltpu.VMEM((2, T, Q), BF16), pltpu.SemaphoreType.DMA((7,))],
        compiler_params=pltpu.CompilerParams(vmem_limit_bytes=10 << 20),
        cost_estimate=pl.CostEstimate(
            flops=4 * W * T * Q, bytes_accessed=4 * T * Q, transcendentals=0
        ),
    )(*pin(lambdas, lam_index, live, sing, u, y))


def rest_kernel(lambdas_h, lam_index_h, live_h, sing_h, u, yt, *rest):
    outs, (lambdas, lam_index, live, sing, us, sems) = rest[:4], rest[4:]
    x, _, _, c = place()
    where = [quarter(name, x, c) for name in ("b", "own")]
    held = (lambdas, lam_index, live, sing)
    copies = [
        pltpu.make_async_copy(r, h, sems.at[i])
        for i, (r, h) in enumerate(zip((lambdas_h, lam_index_h, live_h, sing_h), held))
    ]
    wide = [
        pltpu.make_async_copy(u.at[:, pl.ds(pl.multiple_of(q * Q, Q), Q)], us.at[i], sems.at[4 + i])
        for i, q in enumerate(where)
    ]
    for copy in copies + wide:
        copy.start()
    for copy in copies:
        copy.wait()
    products(where, [outs[:2], outs[2:]], yt, us, wide, slots(live), held)


def rest_call(lambdas, lam_index, live, sing, u, yt):
    return pl.pallas_call(
        rest_kernel,
        out_shape=[jax.ShapeDtypeStruct((BLK, Q), F32)] * 4,
        in_specs=[HBM] * 5 + [VMEM],
        out_specs=[VMEM] * 4,
        scratch_shapes=SMALL + [pltpu.VMEM((2, T, Q), BF16), pltpu.SemaphoreType.DMA((6,))],
        compiler_params=pltpu.CompilerParams(vmem_limit_bytes=10 << 20),
        cost_estimate=pl.CostEstimate(
            flops=4 * W * T * Q, bytes_accessed=4 * T * Q, transcendentals=0
        ),
    )(*pin(lambdas, lam_index, live, sing, u), yt)


def row_kernel(a, b, c, d, out):
    for i, block in enumerate((a, b, c, d)):
        out[i] = block[...]


def row_call(*blocks):
    return pl.pallas_call(
        row_kernel,
        out_shape=jax.ShapeDtypeStruct((NY, Q, BLK), BF16),
        in_specs=[VMEM] * 4,
        out_specs=VMEM,
        compiler_params=pltpu.CompilerParams(vmem_limit_bytes=2 << 20),
        cost_estimate=pl.CostEstimate(
            flops=ROW_COST, bytes_accessed=4 * Q * Q, transcendentals=0
        ),
    )(*blocks)


def pass_kernel(*refs):
    pass


def pass_call(cost, *values):
    n = len(values)
    return pl.pallas_call(
        pass_kernel,
        out_shape=[jax.ShapeDtypeStruct(v.shape, v.dtype) for v in values],
        in_specs=[VMEM] * n,
        out_specs=[VMEM] * n,
        input_output_aliases={i: i for i in range(n)},
        compiler_params=pltpu.CompilerParams(vmem_limit_bytes=1 << 20),
        cost_estimate=pl.CostEstimate(flops=cost, bytes_accessed=1 << 20, transcendentals=0),
    )(*values)


CHUNK = 256


def block_of(distance):
    return jnp.where(distance == 3, 2, jnp.where(distance == 2, 3, distance))


def multiply(q, rows, shards, features):
    _, y, z0, c = place()
    back = (y - q + NY) % NY
    total = None
    for z in range(NZ):
        deep = (z0 - z + NZ) % NZ
        first = c * NY * NZ + block_of(deep) * NY + back
        second = (1 - c) * NY * NZ + block_of(back) * NZ + deep
        left = jnp.concatenate([shards[first, rows, :], shards[second, rows, :]], axis=1)
        columns = slice(z * NC * BLK, (z + 1) * NC * BLK)
        right = jnp.concatenate([f[:, columns] for f in features], axis=0)
        part = lax.dot_general(left, right, (((1,), (1,)), ((), ())), preferred_element_type=F32)
        total = part if total is None else total + part
    return total


def half_kernel(shards, own_0, own_1, other_0, other_1, out):
    x, _, _, c = place()
    for r in range(Q // CHUNK):
        rows = slice(r * CHUNK, (r + 1) * CHUNK)
        out[rows, :] = multiply(x, rows, shards, (own_0, own_1)) + multiply(
            quarter("b", x, c), rows, shards, (other_0, other_1)
        )


def half_call(shards, *features):
    return pl.pallas_call(
        half_kernel,
        out_shape=jax.ShapeDtypeStruct((Q, W), F32),
        in_specs=[VMEM] * 5,
        out_specs=VMEM,
        compiler_params=pltpu.CompilerParams(vmem_limit_bytes=8 << 20),
        cost_estimate=pl.CostEstimate(
            flops=2 * W * 2 * Q * Q, bytes_accessed=2 * Q * 2 * Q, transcendentals=0
        ),
    )(shards, *features)


def spread(out, rows, values, live):
    first, second = slots(live)
    left, right = values[:, :BLK], values[:, BLK:]
    for b in range(NB):
        block = jnp.where(first == b, left, right)
        block = jnp.where(live[b] > 0, block, jnp.zeros_like(block))
        out[rows, b * BLK : (b + 1) * BLK] = block.astype(out.dtype)


def last_kernel(live_h, shards, far_0, far_1, so_far, tests, *rest):
    weights, mine, to_a, to_b, opposite, live, packed, sem = rest
    copy = pltpu.make_async_copy(live_h, live, sem)
    copy.start()
    x, _, _, c = place()
    copy.wait()
    for r in range(Q // CHUNK):
        rows = slice(r * CHUNK, (r + 1) * CHUNK)
        total = so_far[rows, :]
        for i, name in enumerate(("a", "opposite")):
            total = total + multiply(
                quarter(name, x, c), rows, shards, (far_0.at[i], far_1.at[i])
            )
        total = total.astype(BF16)
        packed[rows, :] = total
        spread(weights, rows, total, live)
    count = TEST // NX
    for name, out in (
        ("opposite", opposite),
        ("a", to_a),
        ("b", to_b),
        ("own", mine),
    ):
        q = quarter(name, x, c)
        part = tests[pl.ds(pl.multiple_of(q * count, count), count), :]
        out[...] = jnp.dot(part, packed[...], preferred_element_type=F32).astype(out.dtype)


def last_call(live, shards, far, so_far, tests):
    rows = TEST // NX
    return pl.pallas_call(
        last_kernel,
        out_shape=[
            jax.ShapeDtypeStruct((Q, VD), BF16),
            jax.ShapeDtypeStruct((rows, W), F32),
            jax.ShapeDtypeStruct((rows, W), BF16),
            jax.ShapeDtypeStruct((rows, W), BF16),
            jax.ShapeDtypeStruct((rows, W), BF16),
        ],
        in_specs=[HBM] + [VMEM] * 5,
        out_specs=[VMEM] * 5,
        scratch_shapes=[
            pltpu.SMEM((NB,), jnp.int32),
            pltpu.VMEM((Q, W), BF16),
            pltpu.SemaphoreType.DMA,
        ],
        compiler_params=pltpu.CompilerParams(vmem_limit_bytes=8 << 20),
        cost_estimate=pl.CostEstimate(
            flops=4 * W * Q * Q, bytes_accessed=4 * Q * Q, transcendentals=0
        ),
    )(*pin(live), shards, *far, so_far, tests)


def end_kernel(live_h, mine, a, b, c, out, live, sem):
    copy = pltpu.make_async_copy(live_h, live, sem)
    copy.start()
    total = mine[...] + a[...].astype(F32) + b[...].astype(F32) + c[...].astype(F32)
    copy.wait()
    spread(out, slice(0, TEST // NX), total, live)


def end_call(live, mine, a, b, c):
    return pl.pallas_call(
        end_kernel,
        out_shape=jax.ShapeDtypeStruct((TEST // NX, VD), BF16),
        in_specs=[HBM] + [VMEM] * 4,
        out_specs=VMEM,
        scratch_shapes=[pltpu.SMEM((NB,), jnp.int32), pltpu.SemaphoreType.DMA],
        compiler_params=pltpu.CompilerParams(vmem_limit_bytes=4 << 20),
    )(*pin(live), mine, a, b, c)


def body(u_train, y_train, sing, lambdas, lam_index, live, v_basis, x_test):
    sing = sing.reshape(1, F)
    small = (lambdas, lam_index, live, sing)
    *p_send, yt = start_call(*small, u_train, y_train)
    come = [send(p, PAIR_A) for p in p_send]
    v_basis = after(v_basis, yt)
    near = [send(v_basis, pairs) for pairs in FIRST]
    p_b0, p_b1, p_own0, p_own1 = rest_call(*small, u_train, yt)
    row = row_call(v_basis, *near)
    below = send(row, UP)
    above = send(row, DOWN)
    sum_0 = (p_b0 + come[0][1].astype(F32)).astype(BF16)
    come[1] = after(come[1], sum_0)
    sum_1 = (p_b1 + come[1][1].astype(F32)).astype(BF16)
    from_0, from_1 = send(sum_0, PAIR_B), send(sum_1, PAIR_B)
    own_0 = (p_own0 + come[0][0].astype(F32) + from_0.astype(F32)).astype(BF16)
    from_1 = after(from_1, own_0)
    own_1 = (p_own1 + come[1][0].astype(F32) + from_1.astype(F32)).astype(BF16)
    other_0, other_1 = send(own_0, PAIR_B), send(own_1, PAIR_B)
    both_0 = jnp.stack([own_0, other_0])
    both_1 = jnp.stack([own_1, after(other_1, both_0)])
    (far_0,) = pass_call(LITTLE_COST, send(both_0, PAIR_A))
    far = pass_call(PASS_COST, far_0, send(both_1, PAIR_A))
    below, above = after((below, above), both_1)
    far_a = send(below[:2], UP)
    far_b = send(above[2:], DOWN)
    early = jnp.concatenate([row, below, above])
    early_other = send(early, SWAP)
    late = jnp.concatenate([far_a, far_b])
    late_other = send(late, SWAP)
    shards = jnp.concatenate([early, late, early_other, late_other])
    so_far = half_call(shards, own_0, own_1, other_0, other_1)
    weights, mine, to_a, to_b, opposite = last_call(live, shards, far, so_far, x_test)
    predictions = end_call(
        live, mine, send(opposite, OPPOSITE), send(to_a, PAIR_A), send(to_b, PAIR_B)
    )
    return weights, predictions


def solution(mesh):
    placed = (
        P("tm", None),
        P("tm", "vox"),
        P(),
        P(),
        P("vox"),
        P("vox"),
        P("tm", "vox"),
        P(None, "tm"),
    )
    return jax.shard_map(
        body,
        mesh=mesh,
        in_specs=placed,
        out_specs=(P("tm", "vox"), P("tm", "vox")),
        check_vma=False,
    )
```

```python
import functools

import jax
import jax.numpy as jnp
from jax import lax
from jax.experimental import pallas as pl
from jax.experimental.pallas import tpu as pltpu
from jax.sharding import PartitionSpec as P

F32 = jnp.float32
BF16 = jnp.bfloat16
F = 4096
NLAM = 20
BLK = 128
VD = 384
NB = 3
NS = 2
TEST = 1024
T = 768
Q = 1024
W = NS * BLK
ROW_COST = 20000_000_000
NX = NY = NZ = 4
NC = 2
SMEM = pl.BlockSpec(memory_space=pltpu.SMEM)
VMEM = pl.BlockSpec(memory_space=pltpu.VMEM)
HBM = pl.BlockSpec(memory_space=pltpu.HBM)


def moves(target):
    pairs = []
    for x in range(NX):
        for y in range(NY):
            for z in range(NZ):
                for c in range(NC):
                    tx, ty, tz, tc = target(x, y, z, c)
                    source = ((x * NY + y) * NZ + z) * NC + c
                    goal = (((tx % NX) * NY + ty % NY) * NZ + tz % NZ) * NC + tc % NC
                    pairs.append((source, goal))
    return pairs


PAIR_A = moves(lambda x, y, z, c: (3 - x if c else x ^ 1, y, z, c))
PAIR_B = moves(lambda x, y, z, c: (x ^ 1 if c else 3 - x, y, z, c))
OPPOSITE = moves(lambda x, y, z, c: (x + 2, y, z, c))
SWAP = moves(lambda x, y, z, c: (x, y, z, c + 1))
FIRST = [moves(lambda x, y, z, c, d=d: (x, y + d * (1 - c), z + d * c, c)) for d in (1, 2, 3)]
UP = moves(lambda x, y, z, c: (x, y + c, z + 1 - c, c))
DOWN = moves(lambda x, y, z, c: (x, y - c, z - 1 + c, c))


SECOND = [moves(lambda x, y, z, c, d=d: (x, y + d * c, z + d * (1 - c), c)) for d in (1, 3, 2)]


def pin(*arrays):
    return [pltpu.with_memory_space_constraint(a, pltpu.HBM) for a in arrays]


def send(value, pairs):
    return lax.ppermute(value, ("tm", "vox"), pairs)


def after(value, other):
    return lax.optimization_barrier((value, other))[0]


def place():
    x = lax.axis_index("tm")
    v = lax.axis_index("vox")
    return x, v // (NZ * NC), (v // NC) % NZ, v % NC


def slots(live):
    first = jnp.where(live[0] > 0, 0, jnp.where(live[1] > 0, 1, 2))
    second = jnp.where(live[2] > 0, 2, jnp.where(live[1] > 0, 1, 0))
    return first, second


def quarter(which, x, c):
    flipped = x + 1 - 2 * (x % 2)
    mirrored = NX - 1 - x
    if which == "a":
        return jnp.where(c == 0, flipped, mirrored)
    if which == "b":
        return jnp.where(c == 0, mirrored, flipped)
    if which == "opposite":
        return (x + 2) % NX
    return x


SMALL = [
    pltpu.SMEM((NLAM,), F32),
    pltpu.SMEM((NB,), jnp.int32),
    pltpu.SMEM((NB,), jnp.int32),
    pltpu.VMEM((1, F), F32),
]


def scaled(total, q, picked, lambdas, lam_index, live, sing):
    s = sing[:, pl.ds(pl.multiple_of(q * Q, Q), Q)]
    parts = []
    for j, slot in enumerate(picked):
        scale = s / (s * s + lambdas[lam_index[slot]]) * live[slot].astype(F32)
        parts.append(total[j * BLK : (j + 1) * BLK, :] * scale)
    return parts


def products(where, outs, yt, us, wide, picked, held):
    for i, q in enumerate(where):
        wide[i].wait()
        total = jnp.dot(yt[...], us[i], preferred_element_type=F32)
        for j, part in enumerate(scaled(total, q, picked, *held)):
            outs[i][j][...] = part.astype(outs[i][j].dtype)


def start_kernel(lambdas_h, lam_index_h, live_h, sing_h, u, y, *rest):
    out_0, out_1, yt_out, lambdas, lam_index, live, sing, ys, us, sems = rest
    x, _, _, c = place()
    where = [quarter(name, x, c) for name in ("a", "opposite")]
    held = (lambdas, lam_index, live, sing)
    copies = [
        pltpu.make_async_copy(r, h, sems.at[i])
        for i, (r, h) in enumerate(zip((lambdas_h, lam_index_h, live_h, sing_h), held))
    ]
    whole = pltpu.make_async_copy(y, ys, sems.at[4])
    wide = [
        pltpu.make_async_copy(u.at[:, pl.ds(pl.multiple_of(q * Q, Q), Q)], us.at[i], sems.at[5 + i])
        for i, q in enumerate(where)
    ]
    for copy in copies + [whole] + wide:
        copy.start()
    for copy in copies:
        copy.wait()
    picked = slots(live)
    whole.wait()
    for j, slot in enumerate(picked):
        block = ys[:, pl.ds(pl.multiple_of(slot * BLK, BLK), BLK)]
        yt_out[j * BLK : (j + 1) * BLK, :] = block.T
    outs = [[out_0.at[i], out_1.at[i]] for i in range(2)]
    products(where, outs, yt_out, us, wide, picked, held)


def start_call(lambdas, lam_index, live, sing, u, y):
    return pl.pallas_call(
        start_kernel,
        out_shape=[jax.ShapeDtypeStruct((2, BLK, Q), BF16)] * 2
        + [jax.ShapeDtypeStruct((W, T), BF16)],
        in_specs=[HBM] * 6,
        out_specs=[VMEM] * 3,
        scratch_shapes=SMALL
        + [pltpu.VMEM((T, VD), BF16), pltpu.VMEM((2, T, Q), BF16), pltpu.SemaphoreType.DMA((7,))],
        compiler_params=pltpu.CompilerParams(vmem_limit_bytes=10 << 20),
        cost_estimate=pl.CostEstimate(
            flops=4 * W * T * Q, bytes_accessed=4 * T * Q, transcendentals=0
        ),
    )(*pin(lambdas, lam_index, live, sing, u, y))


def rest_kernel(lambdas_h, lam_index_h, live_h, sing_h, u, yt, *rest):
    outs, (lambdas, lam_index, live, sing, us, sems) = rest[:4], rest[4:]
    x, _, _, c = place()
    where = [quarter(name, x, c) for name in ("b", "own")]
    held = (lambdas, lam_index, live, sing)
    copies = [
        pltpu.make_async_copy(r, h, sems.at[i])
        for i, (r, h) in enumerate(zip((lambdas_h, lam_index_h, live_h, sing_h), held))
    ]
    wide = [
        pltpu.make_async_copy(u.at[:, pl.ds(pl.multiple_of(q * Q, Q), Q)], us.at[i], sems.at[4 + i])
        for i, q in enumerate(where)
    ]
    for copy in copies + wide:
        copy.start()
    for copy in copies:
        copy.wait()
    products(where, [outs[:2], outs[2:]], yt, us, wide, slots(live), held)


def rest_call(lambdas, lam_index, live, sing, u, yt):
    return pl.pallas_call(
        rest_kernel,
        out_shape=[jax.ShapeDtypeStruct((BLK, Q), F32)] * 4,
        in_specs=[HBM] * 5 + [VMEM],
        out_specs=[VMEM] * 4,
        scratch_shapes=SMALL + [pltpu.VMEM((2, T, Q), BF16), pltpu.SemaphoreType.DMA((6,))],
        compiler_params=pltpu.CompilerParams(vmem_limit_bytes=10 << 20),
        cost_estimate=pl.CostEstimate(
            flops=4 * W * T * Q, bytes_accessed=4 * T * Q, transcendentals=0
        ),
    )(*pin(lambdas, lam_index, live, sing, u), yt)


def row_kernel(a, b, c, d, out):
    for i, block in enumerate((a, b, c, d)):
        out[i] = block[...]


def row_call(*blocks):
    return pl.pallas_call(
        row_kernel,
        out_shape=jax.ShapeDtypeStruct((NY, Q, BLK), BF16),
        in_specs=[VMEM] * 4,
        out_specs=VMEM,
        compiler_params=pltpu.CompilerParams(vmem_limit_bytes=2 << 20),
        cost_estimate=pl.CostEstimate(
            flops=ROW_COST, bytes_accessed=4 * Q * Q, transcendentals=0
        ),
    )(*blocks)


def pass_kernel(*refs):
    pass


def hold(cost, *values):
    n = len(values)
    return pl.pallas_call(
        pass_kernel,
        out_shape=[jax.ShapeDtypeStruct(v.shape, v.dtype) for v in values],
        in_specs=[VMEM] * n,
        out_specs=[VMEM] * n,
        input_output_aliases={i: i for i in range(n)},
        compiler_params=pltpu.CompilerParams(vmem_limit_bytes=1 << 20),
        cost_estimate=pl.CostEstimate(flops=cost, bytes_accessed=1 << 20, transcendentals=0),
    )(*values)


CHUNK = 256


def block_of(distance):
    return jnp.where(distance == 3, 2, jnp.where(distance == 2, 3, distance))


def multiply(q, rows, shards, features):
    _, y, z0, c = place()
    back = (y - q + NY) % NY
    total = None
    for z in range(NZ):
        deep = (z0 - z + NZ) % NZ
        first = c * NY * NZ + block_of(deep) * NY + back
        second = (1 - c) * NY * NZ + block_of(back) * NZ + deep
        left = jnp.concatenate([shards[first, rows, :], shards[second, rows, :]], axis=1)
        columns = slice(z * NC * BLK, (z + 1) * NC * BLK)
        right = jnp.concatenate([f[:, columns] for f in features], axis=0)
        part = lax.dot_general(left, right, (((1,), (1,)), ((), ())), preferred_element_type=F32)
        total = part if total is None else total + part
    return total


def half_kernel(shards, own_0, own_1, other_0, other_1, out):
    x, _, _, c = place()
    for r in range(Q // CHUNK):
        rows = slice(r * CHUNK, (r + 1) * CHUNK)
        out[rows, :] = multiply(x, rows, shards, (own_0, own_1)) + multiply(
            quarter("b", x, c), rows, shards, (other_0, other_1)
        )


def half_call(shards, *features):
    return pl.pallas_call(
        half_kernel,
        out_shape=jax.ShapeDtypeStruct((Q, W), F32),
        in_specs=[VMEM] * 5,
        out_specs=VMEM,
        compiler_params=pltpu.CompilerParams(vmem_limit_bytes=8 << 20),
        cost_estimate=pl.CostEstimate(
            flops=6000_000_000, bytes_accessed=2 * Q * 2 * Q, transcendentals=0
        ),
    )(shards, *features)


def spread(out, rows, values, live):
    first, second = slots(live)
    left, right = values[:, :BLK], values[:, BLK:]
    for b in range(NB):
        block = jnp.where(first == b, left, right)
        block = jnp.where(live[b] > 0, block, jnp.zeros_like(block))
        out[rows, b * BLK : (b + 1) * BLK] = block.astype(out.dtype)


def last_kernel(shards, far_0, far_1, so_far, tests, *rest):
    packed, mine, to_a, to_b, opposite = rest
    x, _, _, c = place()
    for r in range(Q // CHUNK):
        rows = slice(r * CHUNK, (r + 1) * CHUNK)
        total = so_far[rows, :]
        for i, name in enumerate(("a", "opposite")):
            total = total + multiply(
                quarter(name, x, c), rows, shards, (far_0.at[i], far_1.at[i])
            )
        total = total.astype(BF16)
        packed[rows, :] = total
    count = TEST // NX
    for name, out in (
        ("opposite", opposite),
        ("a", to_a),
        ("b", to_b),
        ("own", mine),
    ):
        q = quarter(name, x, c)
        part = tests[pl.ds(pl.multiple_of(q * count, count), count), :]
        out[...] = jnp.dot(part, packed[...], preferred_element_type=F32).astype(out.dtype)


def last_call(shards, far, so_far, tests):
    rows = TEST // NX
    return pl.pallas_call(
        last_kernel,
        out_shape=[
            jax.ShapeDtypeStruct((Q, W), BF16),
            jax.ShapeDtypeStruct((rows, W), F32),
            jax.ShapeDtypeStruct((rows, W), BF16),
            jax.ShapeDtypeStruct((rows, W), BF16),
            jax.ShapeDtypeStruct((rows, W), BF16),
        ],
        in_specs=[VMEM] * 5,
        out_specs=[VMEM] * 5,
        compiler_params=pltpu.CompilerParams(vmem_limit_bytes=8 << 20),
        cost_estimate=pl.CostEstimate(
            flops=4 * W * Q * Q, bytes_accessed=4 * Q * Q, transcendentals=0
        ),
    )(shards, *far, so_far, tests)


def spread_kernel(live_h, packed, out, picks, live, sem):
    copy = pltpu.make_async_copy(live_h, live, sem)
    copy.start()
    copy.wait()
    chosen = slots(live)
    for i, slot in enumerate(chosen):
        for b in range(NB):
            here = jnp.where((slot == b) & (live[b] > 0), 1.0, 0.0)
            picks[i, :, b * BLK : (b + 1) * BLK] = jnp.full((8, BLK), here, F32)
    for r in range(Q // CHUNK):
        rows = slice(r * CHUNK, (r + 1) * CHUNK)
        spread(out, rows, packed[rows, :], live)


def spread_call(live, packed):
    return pl.pallas_call(
        spread_kernel,
        out_shape=[
            jax.ShapeDtypeStruct((Q, VD), BF16),
            jax.ShapeDtypeStruct((NS, 8, VD), F32),
        ],
        in_specs=[HBM, VMEM],
        out_specs=[VMEM] * 2,
        scratch_shapes=[pltpu.SMEM((NB,), jnp.int32), pltpu.SemaphoreType.DMA],
        compiler_params=pltpu.CompilerParams(vmem_limit_bytes=4 << 20),
        cost_estimate=pl.CostEstimate(
            flops=1 << 20, bytes_accessed=4 << 20, transcendentals=0
        ),
    )(*pin(live), packed)


def end_sum(picks, mine, *parts):
    total = mine
    for part in parts:
        total = total + part.astype(F32)
    left, right = (jnp.concatenate([h] * NB, axis=1) for h in jnp.split(total, 2, axis=1))
    first, second = (picks[i, :1, :] > 0 for i in range(NS))
    return jnp.where(first, left, jnp.where(second, right, 0.0)).astype(BF16)


def body(u_train, y_train, sing, lambdas, lam_index, live, v_basis, x_test):
    sing = sing.reshape(1, F)
    small = (lambdas, lam_index, live, sing)
    *p_send, yt = start_call(*small, u_train, y_train)
    come_0, come_1 = [send(p, PAIR_A) for p in p_send]
    near = [send(after(v_basis, yt), pairs) for pairs in FIRST]
    p_b0, p_b1, p_own0, p_own1 = rest_call(*small, u_train, yt)
    row = row_call(v_basis, *near)
    come_1 = after(come_1, row)
    sum_0 = (p_b0 + come_0[1].astype(F32)).astype(BF16)
    come_1 = after(come_1, sum_0)
    sum_1 = (p_b1 + come_1[1].astype(F32)).astype(BF16)
    from_0, from_b = send(sum_0, PAIR_B), send(sum_1, PAIR_B)
    ahead = [send(row, pairs) for pairs in SECOND]
    row_other = send(row, SWAP)
    own_0 = (p_own0 + come_0[0].astype(F32) + from_0.astype(F32)).astype(BF16)
    from_1 = after(from_b, own_0)
    own_1 = (p_own1 + come_1[0].astype(F32) + from_1.astype(F32)).astype(BF16)
    other_0, other_1 = send(own_0, PAIR_B), send(own_1, PAIR_B)
    both_0 = jnp.stack([own_0, other_0])
    other_1 = after(other_1, both_0)
    both_1 = jnp.stack([own_1, other_1])
    (far_0,) = hold(500_000_000, send(both_0, PAIR_A))
    far = hold(100000_000_000, far_0, send(both_1, PAIR_A))
    pair = jnp.concatenate(after(ahead[:2], both_1))
    far_row = after(ahead[2], pair)
    (far_row,) = hold(25000_000_000, far_row)
    pair_other = send(pair, SWAP)
    far_other = send(far_row, SWAP)
    shards = jnp.concatenate([row, pair, far_row, row_other, pair_other, far_other])
    so_far = half_call(shards, own_0, own_1, other_0, other_1)
    packed, mine, to_a, to_b, opposite = last_call(shards, far, so_far, x_test)
    weights, picks = spread_call(live, packed)
    predictions = end_sum(
        picks, mine, send(opposite, OPPOSITE), send(to_a, PAIR_A), send(to_b, PAIR_B)
    )
    return weights, predictions


def solution(mesh):
    placed = (
        P("tm", None),
        P("tm", "vox"),
        P(),
        P(),
        P("vox"),
        P("vox"),
        P("tm", "vox"),
        P(None, "tm"),
    )
    return jax.shard_map(
        body,
        mesh=mesh,
        in_specs=placed,
        out_specs=(P("tm", "vox"), P("tm", "vox")),
        check_vma=False,
    )
```

```python
import functools

import jax
import jax.numpy as jnp
from jax import lax
from jax.experimental import pallas as pl
from jax.experimental.pallas import tpu as pltpu
from jax.sharding import PartitionSpec as P

F32 = jnp.float32
BF16 = jnp.bfloat16
F = 4096
NLAM = 20
BLK = 128
VD = 384
NB = 3
NS = 2
TEST = 1024
T = 768
Q = 1024
W = NS * BLK
ROW_COST = 20000_000_000
NX = NY = NZ = 4
NC = 2
SMEM = pl.BlockSpec(memory_space=pltpu.SMEM)
VMEM = pl.BlockSpec(memory_space=pltpu.VMEM)
HBM = pl.BlockSpec(memory_space=pltpu.HBM)


def moves(target):
    pairs = []
    for x in range(NX):
        for y in range(NY):
            for z in range(NZ):
                for c in range(NC):
                    tx, ty, tz, tc = target(x, y, z, c)
                    source = ((x * NY + y) * NZ + z) * NC + c
                    goal = (((tx % NX) * NY + ty % NY) * NZ + tz % NZ) * NC + tc % NC
                    pairs.append((source, goal))
    return pairs


PAIR_A = moves(lambda x, y, z, c: (3 - x if c else x ^ 1, y, z, c))
PAIR_B = moves(lambda x, y, z, c: (x ^ 1 if c else 3 - x, y, z, c))
OPPOSITE = moves(lambda x, y, z, c: (x + 2, y, z, c))
SWAP = moves(lambda x, y, z, c: (x, y, z, c + 1))
FIRST = [moves(lambda x, y, z, c, d=d: (x, y + d * (1 - c), z + d * c, c)) for d in (1, 2, 3)]
UP = moves(lambda x, y, z, c: (x, y + c, z + 1 - c, c))
DOWN = moves(lambda x, y, z, c: (x, y - c, z - 1 + c, c))


SECOND = [moves(lambda x, y, z, c, d=d: (x, y + d * c, z + d * (1 - c), c)) for d in (1, 3, 2)]


def pin(*arrays):
    return [pltpu.with_memory_space_constraint(a, pltpu.HBM) for a in arrays]


def send(value, pairs):
    return lax.ppermute(value, ("tm", "vox"), pairs)


def after(value, other):
    return lax.optimization_barrier((value, other))[0]


def place():
    x = lax.axis_index("tm")
    v = lax.axis_index("vox")
    return x, v // (NZ * NC), (v // NC) % NZ, v % NC


def slots(live):
    first = jnp.where(live[0] > 0, 0, jnp.where(live[1] > 0, 1, 2))
    second = jnp.where(live[2] > 0, 2, jnp.where(live[1] > 0, 1, 0))
    return first, second


def quarter(which, x, c):
    flipped = x + 1 - 2 * (x % 2)
    mirrored = NX - 1 - x
    if which == "a":
        return jnp.where(c == 0, flipped, mirrored)
    if which == "b":
        return jnp.where(c == 0, mirrored, flipped)
    if which == "opposite":
        return (x + 2) % NX
    return x


SMALL = [
    pltpu.SMEM((NLAM,), F32),
    pltpu.SMEM((NB,), jnp.int32),
    pltpu.SMEM((NB,), jnp.int32),
    pltpu.VMEM((1, F), F32),
]


def scaled(total, q, picked, lambdas, lam_index, live, sing):
    s = sing[:, pl.ds(pl.multiple_of(q * Q, Q), Q)]
    parts = []
    for j, slot in enumerate(picked):
        scale = s / (s * s + lambdas[lam_index[slot]]) * live[slot].astype(F32)
        parts.append(total[j * BLK : (j + 1) * BLK, :] * scale)
    return parts


def products(where, outs, yt, us, wide, picked, held):
    for i, q in enumerate(where):
        wide[i].wait()
        total = jnp.dot(yt[...], us[i], preferred_element_type=F32)
        for j, part in enumerate(scaled(total, q, picked, *held)):
            outs[i][j][...] = part.astype(outs[i][j].dtype)


def start_kernel(lambdas_h, lam_index_h, live_h, sing_h, u, y, *rest):
    out_0, out_1, yt_out, lambdas, lam_index, live, sing, ys, us, sems = rest
    x, _, _, c = place()
    where = [quarter(name, x, c) for name in ("a", "opposite")]
    held = (lambdas, lam_index, live, sing)
    copies = [
        pltpu.make_async_copy(r, h, sems.at[i])
        for i, (r, h) in enumerate(zip((lambdas_h, lam_index_h, live_h, sing_h), held))
    ]
    whole = pltpu.make_async_copy(y, ys, sems.at[4])
    wide = [
        pltpu.make_async_copy(u.at[:, pl.ds(pl.multiple_of(q * Q, Q), Q)], us.at[i], sems.at[5 + i])
        for i, q in enumerate(where)
    ]
    for copy in copies + [whole] + wide:
        copy.start()
    for copy in copies:
        copy.wait()
    picked = slots(live)
    whole.wait()
    for j, slot in enumerate(picked):
        block = ys[:, pl.ds(pl.multiple_of(slot * BLK, BLK), BLK)]
        yt_out[j * BLK : (j + 1) * BLK, :] = block.T
    outs = [[out_0.at[i], out_1.at[i]] for i in range(2)]
    products(where, outs, yt_out, us, wide, picked, held)


def start_call(lambdas, lam_index, live, sing, u, y):
    return pl.pallas_call(
        start_kernel,
        out_shape=[jax.ShapeDtypeStruct((2, BLK, Q), BF16)] * 2
        + [jax.ShapeDtypeStruct((W, T), BF16)],
        in_specs=[HBM] * 6,
        out_specs=[VMEM] * 3,
        scratch_shapes=SMALL
        + [pltpu.VMEM((T, VD), BF16), pltpu.VMEM((2, T, Q), BF16), pltpu.SemaphoreType.DMA((7,))],
        compiler_params=pltpu.CompilerParams(vmem_limit_bytes=10 << 20),
        cost_estimate=pl.CostEstimate(
            flops=4 * W * T * Q, bytes_accessed=4 * T * Q, transcendentals=0
        ),
    )(*pin(lambdas, lam_index, live, sing, u, y))


def rest_kernel(lambdas_h, lam_index_h, live_h, sing_h, u, yt, *rest):
    outs, (lambdas, lam_index, live, sing, us, sems) = rest[:4], rest[4:]
    x, _, _, c = place()
    where = [quarter(name, x, c) for name in ("b", "own")]
    held = (lambdas, lam_index, live, sing)
    copies = [
        pltpu.make_async_copy(r, h, sems.at[i])
        for i, (r, h) in enumerate(zip((lambdas_h, lam_index_h, live_h, sing_h), held))
    ]
    wide = [
        pltpu.make_async_copy(u.at[:, pl.ds(pl.multiple_of(q * Q, Q), Q)], us.at[i], sems.at[4 + i])
        for i, q in enumerate(where)
    ]
    for copy in copies + wide:
        copy.start()
    for copy in copies:
        copy.wait()
    products(where, [outs[:2], outs[2:]], yt, us, wide, slots(live), held)


def rest_call(lambdas, lam_index, live, sing, u, yt):
    return pl.pallas_call(
        rest_kernel,
        out_shape=[jax.ShapeDtypeStruct((BLK, Q), F32)] * 4,
        in_specs=[HBM] * 5 + [VMEM],
        out_specs=[VMEM] * 4,
        scratch_shapes=SMALL + [pltpu.VMEM((2, T, Q), BF16), pltpu.SemaphoreType.DMA((6,))],
        compiler_params=pltpu.CompilerParams(vmem_limit_bytes=10 << 20),
        cost_estimate=pl.CostEstimate(
            flops=4 * W * T * Q, bytes_accessed=4 * T * Q, transcendentals=0
        ),
    )(*pin(lambdas, lam_index, live, sing, u), yt)


def row_kernel(a, b, c, d, out):
    for i, block in enumerate((a, b, c, d)):
        out[i] = block[...]


def row_call(*blocks):
    return pl.pallas_call(
        row_kernel,
        out_shape=jax.ShapeDtypeStruct((NY, Q, BLK), BF16),
        in_specs=[VMEM] * 4,
        out_specs=VMEM,
        compiler_params=pltpu.CompilerParams(vmem_limit_bytes=2 << 20),
        cost_estimate=pl.CostEstimate(
            flops=ROW_COST, bytes_accessed=4 * Q * Q, transcendentals=0
        ),
    )(*blocks)


def pass_kernel(*refs):
    pass


def hold(cost, *values):
    n = len(values)
    return pl.pallas_call(
        pass_kernel,
        out_shape=[jax.ShapeDtypeStruct(v.shape, v.dtype) for v in values],
        in_specs=[VMEM] * n,
        out_specs=[VMEM] * n,
        input_output_aliases={i: i for i in range(n)},
        compiler_params=pltpu.CompilerParams(vmem_limit_bytes=1 << 20),
        cost_estimate=pl.CostEstimate(flops=cost, bytes_accessed=1 << 20, transcendentals=0),
    )(*values)


CHUNK = 256


def block_of(distance):
    return jnp.where(distance == 3, 2, jnp.where(distance == 2, 3, distance))


def multiply(q, rows, shards, features):
    _, y, z0, c = place()
    back = (y - q + NY) % NY
    total = None
    for z in range(NZ):
        deep = (z0 - z + NZ) % NZ
        first = c * NY * NZ + block_of(deep) * NY + back
        second = (1 - c) * NY * NZ + block_of(back) * NZ + deep
        left = jnp.concatenate([shards[first, rows, :], shards[second, rows, :]], axis=1)
        columns = slice(z * NC * BLK, (z + 1) * NC * BLK)
        right = jnp.concatenate([f[:, columns] for f in features], axis=0)
        part = lax.dot_general(left, right, (((1,), (1,)), ((), ())), preferred_element_type=F32)
        total = part if total is None else total + part
    return total


def half_kernel(shards, own_0, own_1, other_0, other_1, out):
    x, _, _, c = place()
    for r in range(Q // CHUNK):
        rows = slice(r * CHUNK, (r + 1) * CHUNK)
        out[rows, :] = multiply(x, rows, shards, (own_0, own_1)) + multiply(
            quarter("b", x, c), rows, shards, (other_0, other_1)
        )


def half_call(shards, *features):
    return pl.pallas_call(
        half_kernel,
        out_shape=jax.ShapeDtypeStruct((Q, W), F32),
        in_specs=[VMEM] * 5,
        out_specs=VMEM,
        compiler_params=pltpu.CompilerParams(vmem_limit_bytes=8 << 20),
        cost_estimate=pl.CostEstimate(
            flops=6000_000_000, bytes_accessed=2 * Q * 2 * Q, transcendentals=0
        ),
    )(shards, *features)


def spread(out, rows, values, live):
    first, second = slots(live)
    left, right = values[:, :BLK], values[:, BLK:]
    for b in range(NB):
        block = jnp.where(first == b, left, right)
        block = jnp.where(live[b] > 0, block, jnp.zeros_like(block))
        out[rows, b * BLK : (b + 1) * BLK] = block.astype(out.dtype)


def last_kernel(shards, far_0, far_1, so_far, tests, *rest):
    packed, mine, to_a, to_b, opposite = rest
    x, _, _, c = place()
    for r in range(Q // CHUNK):
        rows = slice(r * CHUNK, (r + 1) * CHUNK)
        total = so_far[rows, :]
        for i, name in enumerate(("a", "opposite")):
            total = total + multiply(
                quarter(name, x, c), rows, shards, (far_0.at[i], far_1.at[i])
            )
        total = total.astype(BF16)
        packed[rows, :] = total
    count = TEST // NX
    for name, out in (
        ("opposite", opposite),
        ("a", to_a),
        ("b", to_b),
        ("own", mine),
    ):
        q = quarter(name, x, c)
        part = tests[pl.ds(pl.multiple_of(q * count, count), count), :]
        out[...] = jnp.dot(part, packed[...], preferred_element_type=F32).astype(out.dtype)


def last_call(shards, far, so_far, tests):
    rows = TEST // NX
    return pl.pallas_call(
        last_kernel,
        out_shape=[
            jax.ShapeDtypeStruct((Q, W), BF16),
            jax.ShapeDtypeStruct((rows, W), F32),
            jax.ShapeDtypeStruct((rows, W), BF16),
            jax.ShapeDtypeStruct((rows, W), BF16),
            jax.ShapeDtypeStruct((rows, W), BF16),
        ],
        in_specs=[VMEM] * 5,
        out_specs=[VMEM] * 5,
        compiler_params=pltpu.CompilerParams(vmem_limit_bytes=8 << 20),
        cost_estimate=pl.CostEstimate(
            flops=4 * W * Q * Q, bytes_accessed=4 * Q * Q, transcendentals=0
        ),
    )(shards, *far, so_far, tests)


def spread_kernel(live_h, packed, out, picks, live, sem):
    copy = pltpu.make_async_copy(live_h, live, sem)
    copy.start()
    copy.wait()
    chosen = slots(live)
    for i, slot in enumerate(chosen):
        for b in range(NB):
            here = jnp.where((slot == b) & (live[b] > 0), 1.0, 0.0)
            picks[i, :, b * BLK : (b + 1) * BLK] = jnp.full((8, BLK), here, F32)
    for r in range(Q // CHUNK):
        rows = slice(r * CHUNK, (r + 1) * CHUNK)
        spread(out, rows, packed[rows, :], live)


def spread_call(live, packed):
    return pl.pallas_call(
        spread_kernel,
        out_shape=[
            jax.ShapeDtypeStruct((Q, VD), BF16),
            jax.ShapeDtypeStruct((NS, 8, VD), F32),
        ],
        in_specs=[HBM, VMEM],
        out_specs=[VMEM] * 2,
        scratch_shapes=[pltpu.SMEM((NB,), jnp.int32), pltpu.SemaphoreType.DMA],
        compiler_params=pltpu.CompilerParams(vmem_limit_bytes=4 << 20),
        cost_estimate=pl.CostEstimate(
            flops=1 << 20, bytes_accessed=4 << 20, transcendentals=0
        ),
    )(*pin(live), packed)


def end_sum(picks, mine, *parts):
    total = mine
    for part in parts:
        total = total + part.astype(F32)
    left, right = (jnp.concatenate([h] * NB, axis=1) for h in jnp.split(total, 2, axis=1))
    first, second = (picks[i, :1, :] > 0 for i in range(NS))
    return jnp.where(first, left, jnp.where(second, right, 0.0)).astype(BF16)


def body(u_train, y_train, sing, lambdas, lam_index, live, v_basis, x_test):
    sing = sing.reshape(1, F)
    small = (lambdas, lam_index, live, sing)
    *p_send, yt = start_call(*small, u_train, y_train)
    come_0, come_1 = [send(p, PAIR_A) for p in p_send]
    near = [send(after(v_basis, yt), pairs) for pairs in FIRST]
    p_b0, p_b1, p_own0, p_own1 = rest_call(*small, u_train, yt)
    row = row_call(v_basis, *near)
    come_1 = after(come_1, row)
    sum_0 = (p_b0 + come_0[1].astype(F32)).astype(BF16)
    come_1 = after(come_1, sum_0)
    sum_1 = (p_b1 + come_1[1].astype(F32)).astype(BF16)
    from_0, from_b = send(sum_0, PAIR_B), send(sum_1, PAIR_B)
    ahead = [send(row, pairs) for pairs in SECOND[:2]]
    own_0 = (p_own0 + come_0[0].astype(F32) + from_0.astype(F32)).astype(BF16)
    across = send(after(row, own_0), SECOND[2])
    from_1 = after(from_b, own_0)
    own_1 = (p_own1 + come_1[0].astype(F32) + from_1.astype(F32)).astype(BF16)
    other_0, other_1 = send(own_0, PAIR_B), send(own_1, PAIR_B)
    both_0 = jnp.stack([own_0, other_0])
    other_1 = after(other_1, both_0)
    both_1 = jnp.stack([own_1, other_1])
    (far_0,) = hold(2000_000_000, send(both_0, PAIR_A))
    far = hold(100000_000_000, far_0, send(both_1, PAIR_A))
    pair = jnp.concatenate(after(ahead[:2], both_1))
    far_row = after(across, pair)
    early = jnp.concatenate([row, pair])
    early_other = send(early, SWAP)
    far_other = send(far_row, SWAP)
    shards = jnp.concatenate([early, far_row, early_other, far_other])
    so_far = half_call(shards, own_0, own_1, other_0, other_1)
    packed, mine, to_a, to_b, opposite = last_call(shards, far, so_far, x_test)
    weights, picks = spread_call(live, packed)
    predictions = end_sum(
        picks, mine, send(opposite, OPPOSITE), send(to_a, PAIR_A), send(to_b, PAIR_B)
    )
    return weights, predictions


def solution(mesh):
    placed = (
        P("tm", None),
        P("tm", "vox"),
        P(),
        P(),
        P("vox"),
        P("vox"),
        P("tm", "vox"),
        P(None, "tm"),
    )
    return jax.shard_map(
        body,
        mesh=mesh,
        in_specs=placed,
        out_specs=(P("tm", "vox"), P("tm", "vox")),
        check_vma=False,
    )
```

```python
import functools

import jax
import jax.numpy as jnp
from jax import lax
from jax.experimental import pallas as pl
from jax.experimental.pallas import tpu as pltpu
from jax.sharding import PartitionSpec as P

F32 = jnp.float32
BF16 = jnp.bfloat16
F = 4096
NLAM = 20
BLK = 128
VD = 384
NB = 3
NS = 2
TEST = 1024
T = 768
Q = 1024
W = NS * BLK
ROW_COST = 20000_000_000
NX = NY = NZ = 4
NC = 2
SMEM = pl.BlockSpec(memory_space=pltpu.SMEM)
VMEM = pl.BlockSpec(memory_space=pltpu.VMEM)
HBM = pl.BlockSpec(memory_space=pltpu.HBM)


def moves(target):
    pairs = []
    for x in range(NX):
        for y in range(NY):
            for z in range(NZ):
                for c in range(NC):
                    tx, ty, tz, tc = target(x, y, z, c)
                    source = ((x * NY + y) * NZ + z) * NC + c
                    goal = (((tx % NX) * NY + ty % NY) * NZ + tz % NZ) * NC + tc % NC
                    pairs.append((source, goal))
    return pairs


PAIR_A = moves(lambda x, y, z, c: (3 - x if c else x ^ 1, y, z, c))
PAIR_B = moves(lambda x, y, z, c: (x ^ 1 if c else 3 - x, y, z, c))
OPPOSITE = moves(lambda x, y, z, c: (x + 2, y, z, c))
SWAP = moves(lambda x, y, z, c: (x, y, z, c + 1))
FIRST = [moves(lambda x, y, z, c, d=d: (x, y + d * (1 - c), z + d * c, c)) for d in (1, 2, 3)]
UP = moves(lambda x, y, z, c: (x, y + c, z + 1 - c, c))
DOWN = moves(lambda x, y, z, c: (x, y - c, z - 1 + c, c))


SECOND = [moves(lambda x, y, z, c, d=d: (x, y + d * c, z + d * (1 - c), c)) for d in (1, 3, 2)]


def pin(*arrays):
    return [pltpu.with_memory_space_constraint(a, pltpu.HBM) for a in arrays]


def send(value, pairs):
    return lax.ppermute(value, ("tm", "vox"), pairs)


def after(value, other):
    return lax.optimization_barrier((value, other))[0]


def place():
    x = lax.axis_index("tm")
    v = lax.axis_index("vox")
    return x, v // (NZ * NC), (v // NC) % NZ, v % NC


def slots(live):
    first = jnp.where(live[0] > 0, 0, jnp.where(live[1] > 0, 1, 2))
    second = jnp.where(live[2] > 0, 2, jnp.where(live[1] > 0, 1, 0))
    return first, second


def quarter(which, x, c):
    flipped = x + 1 - 2 * (x % 2)
    mirrored = NX - 1 - x
    if which == "a":
        return jnp.where(c == 0, flipped, mirrored)
    if which == "b":
        return jnp.where(c == 0, mirrored, flipped)
    if which == "opposite":
        return (x + 2) % NX
    return x


SMALL = [
    pltpu.SMEM((NLAM,), F32),
    pltpu.SMEM((NB,), jnp.int32),
    pltpu.SMEM((NB,), jnp.int32),
    pltpu.VMEM((1, F), F32),
]


def scaled(total, q, picked, lambdas, lam_index, live, sing):
    s = sing[:, pl.ds(pl.multiple_of(q * Q, Q), Q)]
    parts = []
    for j, slot in enumerate(picked):
        scale = s / (s * s + lambdas[lam_index[slot]]) * live[slot].astype(F32)
        parts.append(total[j * BLK : (j + 1) * BLK, :] * scale)
    return parts


def products(where, outs, yt, us, wide, picked, held):
    for i, q in enumerate(where):
        wide[i].wait()
        total = jnp.dot(yt[...], us[i], preferred_element_type=F32)
        for j, part in enumerate(scaled(total, q, picked, *held)):
            outs[i][j][...] = part.astype(outs[i][j].dtype)


def start_kernel(lambdas_h, lam_index_h, live_h, sing_h, u, y, *rest):
    out_0, out_1, yt_out, lambdas, lam_index, live, sing, ys, us, sems = rest
    x, _, _, c = place()
    where = [quarter(name, x, c) for name in ("a", "opposite")]
    held = (lambdas, lam_index, live, sing)
    copies = [
        pltpu.make_async_copy(r, h, sems.at[i])
        for i, (r, h) in enumerate(zip((lambdas_h, lam_index_h, live_h, sing_h), held))
    ]
    whole = pltpu.make_async_copy(y, ys, sems.at[4])
    wide = [
        pltpu.make_async_copy(u.at[:, pl.ds(pl.multiple_of(q * Q, Q), Q)], us.at[i], sems.at[5 + i])
        for i, q in enumerate(where)
    ]
    for copy in copies + [whole] + wide:
        copy.start()
    for copy in copies:
        copy.wait()
    picked = slots(live)
    whole.wait()
    for j, slot in enumerate(picked):
        block = ys[:, pl.ds(pl.multiple_of(slot * BLK, BLK), BLK)]
        yt_out[j * BLK : (j + 1) * BLK, :] = block.T
    outs = [[out_0.at[i], out_1.at[i]] for i in range(2)]
    products(where, outs, yt_out, us, wide, picked, held)


def start_call(lambdas, lam_index, live, sing, u, y):
    return pl.pallas_call(
        start_kernel,
        out_shape=[jax.ShapeDtypeStruct((2, BLK, Q), BF16)] * 2
        + [jax.ShapeDtypeStruct((W, T), BF16)],
        in_specs=[HBM] * 6,
        out_specs=[VMEM] * 3,
        scratch_shapes=SMALL
        + [pltpu.VMEM((T, VD), BF16), pltpu.VMEM((2, T, Q), BF16), pltpu.SemaphoreType.DMA((7,))],
        compiler_params=pltpu.CompilerParams(vmem_limit_bytes=10 << 20),
        cost_estimate=pl.CostEstimate(
            flops=4 * W * T * Q, bytes_accessed=4 * T * Q, transcendentals=0
        ),
    )(*pin(lambdas, lam_index, live, sing, u, y))


def rest_kernel(lambdas_h, lam_index_h, live_h, sing_h, u, yt, *rest):
    outs, (lambdas, lam_index, live, sing, us, sems) = rest[:4], rest[4:]
    x, _, _, c = place()
    where = [quarter(name, x, c) for name in ("b", "own")]
    held = (lambdas, lam_index, live, sing)
    copies = [
        pltpu.make_async_copy(r, h, sems.at[i])
        for i, (r, h) in enumerate(zip((lambdas_h, lam_index_h, live_h, sing_h), held))
    ]
    wide = [
        pltpu.make_async_copy(u.at[:, pl.ds(pl.multiple_of(q * Q, Q), Q)], us.at[i], sems.at[4 + i])
        for i, q in enumerate(where)
    ]
    for copy in copies + wide:
        copy.start()
    for copy in copies:
        copy.wait()
    products(where, [outs[:2], outs[2:]], yt, us, wide, slots(live), held)


def rest_call(lambdas, lam_index, live, sing, u, yt):
    return pl.pallas_call(
        rest_kernel,
        out_shape=[jax.ShapeDtypeStruct((BLK, Q), F32)] * 4,
        in_specs=[HBM] * 5 + [VMEM],
        out_specs=[VMEM] * 4,
        scratch_shapes=SMALL + [pltpu.VMEM((2, T, Q), BF16), pltpu.SemaphoreType.DMA((6,))],
        compiler_params=pltpu.CompilerParams(vmem_limit_bytes=10 << 20),
        cost_estimate=pl.CostEstimate(
            flops=4 * W * T * Q, bytes_accessed=4 * T * Q, transcendentals=0
        ),
    )(*pin(lambdas, lam_index, live, sing, u), yt)


def row_kernel(a, b, c, d, out):
    for i, block in enumerate((a, b, c, d)):
        out[i] = block[...]


def row_call(*blocks):
    return pl.pallas_call(
        row_kernel,
        out_shape=jax.ShapeDtypeStruct((NY, Q, BLK), BF16),
        in_specs=[VMEM] * 4,
        out_specs=VMEM,
        compiler_params=pltpu.CompilerParams(vmem_limit_bytes=2 << 20),
        cost_estimate=pl.CostEstimate(
            flops=ROW_COST, bytes_accessed=4 * Q * Q, transcendentals=0
        ),
    )(*blocks)


def pass_kernel(*refs):
    pass


def hold(cost, *values):
    n = len(values)
    return pl.pallas_call(
        pass_kernel,
        out_shape=[jax.ShapeDtypeStruct(v.shape, v.dtype) for v in values],
        in_specs=[VMEM] * n,
        out_specs=[VMEM] * n,
        input_output_aliases={i: i for i in range(n)},
        compiler_params=pltpu.CompilerParams(vmem_limit_bytes=1 << 20),
        cost_estimate=pl.CostEstimate(flops=cost, bytes_accessed=1 << 20, transcendentals=0),
    )(*values)


CHUNK = 256


def block_of(distance):
    return jnp.where(distance == 3, 2, jnp.where(distance == 2, 3, distance))


def multiply(q, rows, shards, features):
    _, y, z0, c = place()
    back = (y - q + NY) % NY
    total = None
    for z in range(NZ):
        deep = (z0 - z + NZ) % NZ
        first = c * NY * NZ + block_of(deep) * NY + back
        second = (1 - c) * NY * NZ + block_of(back) * NZ + deep
        left = jnp.concatenate([shards[first, rows, :], shards[second, rows, :]], axis=1)
        columns = slice(z * NC * BLK, (z + 1) * NC * BLK)
        right = jnp.concatenate([f[:, columns] for f in features], axis=0)
        part = lax.dot_general(left, right, (((1,), (1,)), ((), ())), preferred_element_type=F32)
        total = part if total is None else total + part
    return total


def spread(out, rows, values, live):
    first, second = slots(live)
    left, right = values[:, :BLK], values[:, BLK:]
    for b in range(NB):
        block = jnp.where(first == b, left, right)
        block = jnp.where(live[b] > 0, block, jnp.zeros_like(block))
        out[rows, b * BLK : (b + 1) * BLK] = block.astype(out.dtype)


def last_kernel(shards, far_0, far_1, own_0, own_1, other_0, other_1, tests, *rest):
    packed, mine, to_a, to_b, opposite = rest
    x, _, _, c = place()
    for r in range(Q // CHUNK):
        rows = slice(r * CHUNK, (r + 1) * CHUNK)
        total = multiply(x, rows, shards, (own_0, own_1))
        total = total + multiply(quarter("b", x, c), rows, shards, (other_0, other_1))
        for i, name in enumerate(("a", "opposite")):
            total = total + multiply(
                quarter(name, x, c), rows, shards, (far_0.at[i], far_1.at[i])
            )
        total = total.astype(BF16)
        packed[rows, :] = total
    count = TEST // NX
    for name, out in (
        ("opposite", opposite),
        ("a", to_a),
        ("b", to_b),
        ("own", mine),
    ):
        q = quarter(name, x, c)
        part = tests[pl.ds(pl.multiple_of(q * count, count), count), :]
        out[...] = jnp.dot(part, packed[...], preferred_element_type=F32).astype(out.dtype)


def last_call(shards, far, near, tests):
    rows = TEST // NX
    return pl.pallas_call(
        last_kernel,
        out_shape=[
            jax.ShapeDtypeStruct((Q, W), BF16),
            jax.ShapeDtypeStruct((rows, W), F32),
            jax.ShapeDtypeStruct((rows, W), BF16),
            jax.ShapeDtypeStruct((rows, W), BF16),
            jax.ShapeDtypeStruct((rows, W), BF16),
        ],
        in_specs=[VMEM] * 8,
        out_specs=[VMEM] * 5,
        compiler_params=pltpu.CompilerParams(vmem_limit_bytes=8 << 20),
        cost_estimate=pl.CostEstimate(
            flops=4 * W * Q * Q, bytes_accessed=4 * Q * Q, transcendentals=0
        ),
    )(shards, *far, *near, tests)


def spread_kernel(live_h, packed, out, picks, live, sem):
    copy = pltpu.make_async_copy(live_h, live, sem)
    copy.start()
    copy.wait()
    chosen = slots(live)
    for i, slot in enumerate(chosen):
        for b in range(NB):
            here = jnp.where((slot == b) & (live[b] > 0), 1.0, 0.0)
            picks[i, :, b * BLK : (b + 1) * BLK] = jnp.full((8, BLK), here, F32)
    for r in range(Q // CHUNK):
        rows = slice(r * CHUNK, (r + 1) * CHUNK)
        spread(out, rows, packed[rows, :], live)


def spread_call(live, packed):
    return pl.pallas_call(
        spread_kernel,
        out_shape=[
            jax.ShapeDtypeStruct((Q, VD), BF16),
            jax.ShapeDtypeStruct((NS, 8, VD), F32),
        ],
        in_specs=[HBM, VMEM],
        out_specs=[VMEM] * 2,
        scratch_shapes=[pltpu.SMEM((NB,), jnp.int32), pltpu.SemaphoreType.DMA],
        compiler_params=pltpu.CompilerParams(vmem_limit_bytes=4 << 20),
        cost_estimate=pl.CostEstimate(
            flops=1 << 20, bytes_accessed=4 << 20, transcendentals=0
        ),
    )(*pin(live), packed)


def end_sum(picks, mine, *parts):
    total = mine
    for part in parts:
        total = total + part.astype(F32)
    left, right = (jnp.concatenate([h] * NB, axis=1) for h in jnp.split(total, 2, axis=1))
    first, second = (picks[i, :1, :] > 0 for i in range(NS))
    return jnp.where(first, left, jnp.where(second, right, 0.0)).astype(BF16)


def body(u_train, y_train, sing, lambdas, lam_index, live, v_basis, x_test):
    sing = sing.reshape(1, F)
    small = (lambdas, lam_index, live, sing)
    *p_send, yt = start_call(*small, u_train, y_train)
    come_0, come_1 = [send(p, PAIR_A) for p in p_send]
    near = [send(after(v_basis, yt), pairs) for pairs in FIRST]
    p_b0, p_b1, p_own0, p_own1 = rest_call(*small, u_train, yt)
    row = row_call(v_basis, *near)
    come_1 = after(come_1, row)
    sum_0 = (p_b0 + come_0[1].astype(F32)).astype(BF16)
    come_1 = after(come_1, sum_0)
    sum_1 = (p_b1 + come_1[1].astype(F32)).astype(BF16)
    from_0, from_b = send(sum_0, PAIR_B), send(sum_1, PAIR_B)
    ahead = [send(row, pairs) for pairs in SECOND[:2]]
    own_0 = (p_own0 + come_0[0].astype(F32) + from_0.astype(F32)).astype(BF16)
    across = send(after(row, own_0), SECOND[2])
    from_1 = after(from_b, own_0)
    own_1 = (p_own1 + come_1[0].astype(F32) + from_1.astype(F32)).astype(BF16)
    other_0, other_1 = send(own_0, PAIR_B), send(own_1, PAIR_B)
    both_0 = jnp.stack([own_0, other_0])
    other_1 = after(other_1, both_0)
    both_1 = jnp.stack([own_1, other_1])
    (far_0,) = hold(2000_000_000, send(both_0, PAIR_A))
    far = hold(100000_000_000, far_0, send(both_1, PAIR_A))
    pair = jnp.concatenate(after(ahead[:2], both_1))
    far_row = after(across, pair)
    early = jnp.concatenate([row, pair])
    early_other = send(early, SWAP)
    far_other = send(far_row, SWAP)
    shards = jnp.concatenate([early, far_row, early_other, far_other])
    packed, mine, to_a, to_b, opposite = last_call(shards, far, (own_0, own_1, other_0, other_1), x_test)
    weights, picks = spread_call(live, packed)
    predictions = end_sum(
        picks, mine, send(opposite, OPPOSITE), send(to_a, PAIR_A), send(to_b, PAIR_B)
    )
    return weights, predictions


def solution(mesh):
    placed = (
        P("tm", None),
        P("tm", "vox"),
        P(),
        P(),
        P("vox"),
        P("vox"),
        P("tm", "vox"),
        P(None, "tm"),
    )
    return jax.shard_map(
        body,
        mesh=mesh,
        in_specs=placed,
        out_specs=(P("tm", "vox"), P("tm", "vox")),
        check_vma=False,
    )
```

```python
import functools

import jax
import jax.numpy as jnp
from jax import lax
from jax.experimental import pallas as pl
from jax.experimental.pallas import tpu as pltpu
from jax.sharding import PartitionSpec as P

F32 = jnp.float32
BF16 = jnp.bfloat16
F = 4096
NLAM = 20
BLK = 128
VD = 384
NB = 3
NS = 2
TEST = 1024
T = 768
Q = 1024
W = NS * BLK
ROW_COST = 20000_000_000
NX = NY = NZ = 4
NC = 2
SMEM = pl.BlockSpec(memory_space=pltpu.SMEM)
VMEM = pl.BlockSpec(memory_space=pltpu.VMEM)
HBM = pl.BlockSpec(memory_space=pltpu.HBM)


def moves(target):
    pairs = []
    for x in range(NX):
        for y in range(NY):
            for z in range(NZ):
                for c in range(NC):
                    tx, ty, tz, tc = target(x, y, z, c)
                    source = ((x * NY + y) * NZ + z) * NC + c
                    goal = (((tx % NX) * NY + ty % NY) * NZ + tz % NZ) * NC + tc % NC
                    pairs.append((source, goal))
    return pairs


PAIR_A = moves(lambda x, y, z, c: (3 - x if c else x ^ 1, y, z, c))
PAIR_B = moves(lambda x, y, z, c: (x ^ 1 if c else 3 - x, y, z, c))
OPPOSITE = moves(lambda x, y, z, c: (x + 2, y, z, c))
SWAP = moves(lambda x, y, z, c: (x, y, z, c + 1))
FIRST = [moves(lambda x, y, z, c, d=d: (x, y + d * (1 - c), z + d * c, c)) for d in (1, 2, 3)]
UP = moves(lambda x, y, z, c: (x, y + c, z + 1 - c, c))
DOWN = moves(lambda x, y, z, c: (x, y - c, z - 1 + c, c))


SECOND = [moves(lambda x, y, z, c, d=d: (x, y + d * c, z + d * (1 - c), c)) for d in (1, 3, 2)]


def pin(*arrays):
    return [pltpu.with_memory_space_constraint(a, pltpu.HBM) for a in arrays]


def send(value, pairs):
    return lax.ppermute(value, ("tm", "vox"), pairs)


def after(value, other):
    return lax.optimization_barrier((value, other))[0]


def place():
    x = lax.axis_index("tm")
    v = lax.axis_index("vox")
    return x, v // (NZ * NC), (v // NC) % NZ, v % NC


def slots(live):
    first = jnp.where(live[0] > 0, 0, jnp.where(live[1] > 0, 1, 2))
    second = jnp.where(live[2] > 0, 2, jnp.where(live[1] > 0, 1, 0))
    return first, second


def quarter(which, x, c):
    flipped = x + 1 - 2 * (x % 2)
    mirrored = NX - 1 - x
    if which == "a":
        return jnp.where(c == 0, flipped, mirrored)
    if which == "b":
        return jnp.where(c == 0, mirrored, flipped)
    if which == "opposite":
        return (x + 2) % NX
    return x


SMALL = [
    pltpu.SMEM((NLAM,), F32),
    pltpu.SMEM((NB,), jnp.int32),
    pltpu.SMEM((NB,), jnp.int32),
    pltpu.VMEM((1, F), F32),
]


def scaled(total, q, picked, lambdas, lam_index, live, sing):
    s = sing[:, pl.ds(pl.multiple_of(q * Q, Q), Q)]
    parts = []
    for j, slot in enumerate(picked):
        scale = s / (s * s + lambdas[lam_index[slot]]) * live[slot].astype(F32)
        parts.append(total[j * BLK : (j + 1) * BLK, :] * scale)
    return parts


def products(where, outs, yt, us, wide, picked, held):
    for i, q in enumerate(where):
        wide[i].wait()
        total = jnp.dot(yt[...], us[i], preferred_element_type=F32)
        for j, part in enumerate(scaled(total, q, picked, *held)):
            outs[i][j][...] = part.astype(outs[i][j].dtype)


def start_kernel(lambdas_h, lam_index_h, live_h, sing_h, u, y, *rest):
    out_0, out_1, yt_out, lambdas, lam_index, live, sing, ys, us, sems = rest
    x, _, _, c = place()
    where = [quarter(name, x, c) for name in ("a", "opposite")]
    held = (lambdas, lam_index, live, sing)
    copies = [
        pltpu.make_async_copy(r, h, sems.at[i])
        for i, (r, h) in enumerate(zip((lambdas_h, lam_index_h, live_h, sing_h), held))
    ]
    whole = pltpu.make_async_copy(y, ys, sems.at[4])
    wide = [
        pltpu.make_async_copy(u.at[:, pl.ds(pl.multiple_of(q * Q, Q), Q)], us.at[i], sems.at[5 + i])
        for i, q in enumerate(where)
    ]
    for copy in copies + [whole] + wide:
        copy.start()
    for copy in copies:
        copy.wait()
    picked = slots(live)
    whole.wait()
    for j, slot in enumerate(picked):
        block = ys[:, pl.ds(pl.multiple_of(slot * BLK, BLK), BLK)]
        yt_out[j * BLK : (j + 1) * BLK, :] = block.T
    outs = [[out_0.at[i], out_1.at[i]] for i in range(2)]
    products(where, outs, yt_out, us, wide, picked, held)


def start_call(lambdas, lam_index, live, sing, u, y):
    return pl.pallas_call(
        start_kernel,
        out_shape=[jax.ShapeDtypeStruct((2, BLK, Q), BF16)] * 2
        + [jax.ShapeDtypeStruct((W, T), BF16)],
        in_specs=[HBM] * 6,
        out_specs=[VMEM] * 3,
        scratch_shapes=SMALL
        + [pltpu.VMEM((T, VD), BF16), pltpu.VMEM((2, T, Q), BF16), pltpu.SemaphoreType.DMA((7,))],
        compiler_params=pltpu.CompilerParams(vmem_limit_bytes=10 << 20),
        cost_estimate=pl.CostEstimate(
            flops=4 * W * T * Q, bytes_accessed=4 * T * Q, transcendentals=0
        ),
    )(*pin(lambdas, lam_index, live, sing, u, y))


def rest_kernel(lambdas_h, lam_index_h, live_h, sing_h, u, yt, *rest):
    outs, (lambdas, lam_index, live, sing, us, sems) = rest[:4], rest[4:]
    x, _, _, c = place()
    where = [quarter(name, x, c) for name in ("b", "own")]
    held = (lambdas, lam_index, live, sing)
    copies = [
        pltpu.make_async_copy(r, h, sems.at[i])
        for i, (r, h) in enumerate(zip((lambdas_h, lam_index_h, live_h, sing_h), held))
    ]
    wide = [
        pltpu.make_async_copy(u.at[:, pl.ds(pl.multiple_of(q * Q, Q), Q)], us.at[i], sems.at[4 + i])
        for i, q in enumerate(where)
    ]
    for copy in copies + wide:
        copy.start()
    for copy in copies:
        copy.wait()
    products(where, [outs[:2], outs[2:]], yt, us, wide, slots(live), held)


def rest_call(lambdas, lam_index, live, sing, u, yt):
    return pl.pallas_call(
        rest_kernel,
        out_shape=[jax.ShapeDtypeStruct((BLK, Q), F32)] * 4,
        in_specs=[HBM] * 5 + [VMEM],
        out_specs=[VMEM] * 4,
        scratch_shapes=SMALL + [pltpu.VMEM((2, T, Q), BF16), pltpu.SemaphoreType.DMA((6,))],
        compiler_params=pltpu.CompilerParams(vmem_limit_bytes=10 << 20),
        cost_estimate=pl.CostEstimate(
            flops=4 * W * T * Q, bytes_accessed=4 * T * Q, transcendentals=0
        ),
    )(*pin(lambdas, lam_index, live, sing, u), yt)


def row_kernel(a, b, c, d, out):
    for i, block in enumerate((a, b, c, d)):
        out[i] = block[...]


def row_call(*blocks):
    return pl.pallas_call(
        row_kernel,
        out_shape=jax.ShapeDtypeStruct((NY, Q, BLK), BF16),
        in_specs=[VMEM] * 4,
        out_specs=VMEM,
        compiler_params=pltpu.CompilerParams(vmem_limit_bytes=2 << 20),
        cost_estimate=pl.CostEstimate(
            flops=ROW_COST, bytes_accessed=4 * Q * Q, transcendentals=0
        ),
    )(*blocks)


def pass_kernel(*refs):
    pass


def hold(cost, *values):
    n = len(values)
    return pl.pallas_call(
        pass_kernel,
        out_shape=[jax.ShapeDtypeStruct(v.shape, v.dtype) for v in values],
        in_specs=[VMEM] * n,
        out_specs=[VMEM] * n,
        input_output_aliases={i: i for i in range(n)},
        compiler_params=pltpu.CompilerParams(vmem_limit_bytes=1 << 20),
        cost_estimate=pl.CostEstimate(flops=cost, bytes_accessed=1 << 20, transcendentals=0),
    )(*values)


CHUNK = 256


def block_of(distance):
    return jnp.where(distance == 3, 2, jnp.where(distance == 2, 3, distance))


def multiply(q, rows, shards, features):
    _, y, z0, c = place()
    back = (y - q + NY) % NY
    total = None
    for z in range(NZ):
        deep = (z0 - z + NZ) % NZ
        first = c * NY * NZ + block_of(deep) * NY + back
        second = (1 - c) * NY * NZ + block_of(back) * NZ + deep
        left = jnp.concatenate([shards[first, rows, :], shards[second, rows, :]], axis=1)
        columns = slice(z * NC * BLK, (z + 1) * NC * BLK)
        right = jnp.concatenate([f[:, columns] for f in features], axis=0)
        part = lax.dot_general(left, right, (((1,), (1,)), ((), ())), preferred_element_type=F32)
        total = part if total is None else total + part
    return total


def spread(out, rows, values, live):
    first, second = slots(live)
    left, right = values[:, :BLK], values[:, BLK:]
    for b in range(NB):
        block = jnp.where(first == b, left, right)
        block = jnp.where(live[b] > 0, block, jnp.zeros_like(block))
        out[rows, b * BLK : (b + 1) * BLK] = block.astype(out.dtype)


def last_kernel(shards, far_0, far_1, own_0, own_1, other_0, other_1, tests, *rest):
    packed, mine, to_a, to_b, opposite = rest
    x, _, _, c = place()
    for r in range(Q // CHUNK):
        rows = slice(r * CHUNK, (r + 1) * CHUNK)
        total = multiply(x, rows, shards, (own_0, own_1))
        total = total + multiply(quarter("b", x, c), rows, shards, (other_0, other_1))
        for i, name in enumerate(("a", "opposite")):
            total = total + multiply(
                quarter(name, x, c), rows, shards, (far_0.at[i], far_1.at[i])
            )
        total = total.astype(BF16)
        packed[rows, :] = total
    count = TEST // NX
    for name, out in (
        ("opposite", opposite),
        ("a", to_a),
        ("b", to_b),
        ("own", mine),
    ):
        q = quarter(name, x, c)
        part = tests[pl.ds(pl.multiple_of(q * count, count), count), :]
        out[...] = jnp.dot(part, packed[...], preferred_element_type=F32).astype(out.dtype)


def last_call(shards, far, near, tests):
    rows = TEST // NX
    return pl.pallas_call(
        last_kernel,
        out_shape=[
            jax.ShapeDtypeStruct((Q, W), BF16),
            jax.ShapeDtypeStruct((rows, W), F32),
            jax.ShapeDtypeStruct((rows, W), BF16),
            jax.ShapeDtypeStruct((rows, W), BF16),
            jax.ShapeDtypeStruct((rows, W), BF16),
        ],
        in_specs=[VMEM] * 8,
        out_specs=[VMEM] * 5,
        compiler_params=pltpu.CompilerParams(vmem_limit_bytes=8 << 20),
        cost_estimate=pl.CostEstimate(
            flops=4 * W * Q * Q, bytes_accessed=4 * Q * Q, transcendentals=0
        ),
    )(shards, *far, *near, tests)


def spread_kernel(live_h, packed, out, picks, live, sem):
    copy = pltpu.make_async_copy(live_h, live, sem)
    copy.start()
    copy.wait()
    chosen = slots(live)
    for i, slot in enumerate(chosen):
        for b in range(NB):
            here = jnp.where((slot == b) & (live[b] > 0), 1.0, 0.0)
            picks[i, :, b * BLK : (b + 1) * BLK] = jnp.full((8, BLK), here, F32)
    for r in range(Q // CHUNK):
        rows = slice(r * CHUNK, (r + 1) * CHUNK)
        spread(out, rows, packed[rows, :], live)


def spread_call(live, packed):
    return pl.pallas_call(
        spread_kernel,
        out_shape=[
            jax.ShapeDtypeStruct((Q, VD), BF16),
            jax.ShapeDtypeStruct((NS, 8, VD), F32),
        ],
        in_specs=[HBM, VMEM],
        out_specs=[VMEM] * 2,
        scratch_shapes=[pltpu.SMEM((NB,), jnp.int32), pltpu.SemaphoreType.DMA],
        compiler_params=pltpu.CompilerParams(vmem_limit_bytes=4 << 20),
        cost_estimate=pl.CostEstimate(
            flops=1 << 20, bytes_accessed=4 << 20, transcendentals=0
        ),
    )(*pin(live), packed)


def end_sum(picks, mine, *parts):
    total = mine
    for part in parts:
        total = total + part.astype(F32)
    left, right = (jnp.concatenate([h] * NB, axis=1) for h in jnp.split(total, 2, axis=1))
    first, second = (picks[i, :1, :] > 0 for i in range(NS))
    return jnp.where(first, left, jnp.where(second, right, 0.0)).astype(BF16)


def body(u_train, y_train, sing, lambdas, lam_index, live, v_basis, x_test):
    sing = sing.reshape(1, F)
    small = (lambdas, lam_index, live, sing)
    *p_send, yt = start_call(*small, u_train, y_train)
    come_0, come_1 = [send(p, PAIR_A) for p in p_send]
    near = [send(after(v_basis, yt), pairs) for pairs in FIRST]
    p_b0, p_b1, p_own0, p_own1 = rest_call(*small, u_train, yt)
    row = row_call(v_basis, *near)
    come_1 = after(come_1, row)
    sum_0 = (p_b0 + come_0[1].astype(F32)).astype(BF16)
    come_1 = after(come_1, sum_0)
    sum_1 = (p_b1 + come_1[1].astype(F32)).astype(BF16)
    from_0, from_b = send(sum_0, PAIR_B), send(sum_1, PAIR_B)
    ahead = [send(row, pairs) for pairs in SECOND[:2]]
    own_0 = (p_own0 + come_0[0].astype(F32) + from_0.astype(F32)).astype(BF16)
    across = send(after(row, own_0), SECOND[2])
    from_1 = after(from_b, own_0)
    own_1 = (p_own1 + come_1[0].astype(F32) + from_1.astype(F32)).astype(BF16)
    other_0, other_1 = send(own_0, PAIR_B), send(own_1, PAIR_B)
    both_0 = jnp.stack([own_0, other_0])
    other_1 = after(other_1, both_0)
    both_1 = jnp.stack([own_1, other_1])
    (far_0,) = hold(2000_000_000, send(both_0, PAIR_A))
    far = hold(100000_000_000, far_0, send(both_1, PAIR_A))
    pair = jnp.concatenate(after(ahead[:2], both_1))
    far_row = after(across, pair)
    early = jnp.concatenate([row, pair])
    early_other = send(early, SWAP)
    far_other = send(far_row, SWAP)
    shards = jnp.concatenate([early, far_row, early_other, far_other])
    packed, mine, to_a, to_b, opposite = last_call(shards, far, (own_0, own_1, other_0, other_1), x_test)
    weights, picks = spread_call(live, packed)
    predictions = end_sum(
        picks, mine, send(to_b, PAIR_B), send(to_a, PAIR_A), send(opposite, OPPOSITE)
    )
    return weights, predictions


def solution(mesh):
    placed = (
        P("tm", None),
        P("tm", "vox"),
        P(),
        P(),
        P("vox"),
        P("vox"),
        P("tm", "vox"),
        P(None, "tm"),
    )
    return jax.shard_map(
        body,
        mesh=mesh,
        in_specs=placed,
        out_specs=(P("tm", "vox"), P("tm", "vox")),
        check_vma=False,
    )
```

```python
import functools

import jax
import jax.numpy as jnp
from jax import lax
from jax.experimental import pallas as pl
from jax.experimental.pallas import tpu as pltpu
from jax.sharding import PartitionSpec as P

F32 = jnp.float32
BF16 = jnp.bfloat16
F = 4096
NLAM = 20
BLK = 128
VD = 384
NB = 3
NS = 2
TEST = 1024
T = 768
Q = 1024
W = NS * BLK
ROW_COST = 20000_000_000
NX = NY = NZ = 4
NC = 2
SMEM = pl.BlockSpec(memory_space=pltpu.SMEM)
VMEM = pl.BlockSpec(memory_space=pltpu.VMEM)
HBM = pl.BlockSpec(memory_space=pltpu.HBM)


def moves(target):
    pairs = []
    for x in range(NX):
        for y in range(NY):
            for z in range(NZ):
                for c in range(NC):
                    tx, ty, tz, tc = target(x, y, z, c)
                    source = ((x * NY + y) * NZ + z) * NC + c
                    goal = (((tx % NX) * NY + ty % NY) * NZ + tz % NZ) * NC + tc % NC
                    pairs.append((source, goal))
    return pairs


PAIR_A = moves(lambda x, y, z, c: (3 - x if c else x ^ 1, y, z, c))
PAIR_B = moves(lambda x, y, z, c: (x ^ 1 if c else 3 - x, y, z, c))
OPPOSITE = moves(lambda x, y, z, c: (x + 2, y, z, c))
SWAP = moves(lambda x, y, z, c: (x, y, z, c + 1))
FIRST = [moves(lambda x, y, z, c, d=d: (x, y + d * (1 - c), z + d * c, c)) for d in (1, 2, 3)]
UP = moves(lambda x, y, z, c: (x, y + c, z + 1 - c, c))
DOWN = moves(lambda x, y, z, c: (x, y - c, z - 1 + c, c))


SECOND = [moves(lambda x, y, z, c, d=d: (x, y + d * c, z + d * (1 - c), c)) for d in (1, 3, 2)]


def pin(*arrays):
    return [pltpu.with_memory_space_constraint(a, pltpu.HBM) for a in arrays]


def send(value, pairs):
    return lax.ppermute(value, ("tm", "vox"), pairs)


def after(value, other):
    return lax.optimization_barrier((value, other))[0]


def place():
    x = lax.axis_index("tm")
    v = lax.axis_index("vox")
    return x, v // (NZ * NC), (v // NC) % NZ, v % NC


def slots(live):
    first = jnp.where(live[0] > 0, 0, jnp.where(live[1] > 0, 1, 2))
    second = jnp.where(live[2] > 0, 2, jnp.where(live[1] > 0, 1, 0))
    return first, second


def quarter(which, x, c):
    flipped = x + 1 - 2 * (x % 2)
    mirrored = NX - 1 - x
    if which == "a":
        return jnp.where(c == 0, flipped, mirrored)
    if which == "b":
        return jnp.where(c == 0, mirrored, flipped)
    if which == "opposite":
        return (x + 2) % NX
    return x


SMALL = [
    pltpu.SMEM((NLAM,), F32),
    pltpu.SMEM((NB,), jnp.int32),
    pltpu.SMEM((NB,), jnp.int32),
    pltpu.VMEM((1, F), F32),
]


def scaled(total, q, picked, lambdas, lam_index, live, sing):
    s = sing[:, pl.ds(pl.multiple_of(q * Q, Q), Q)]
    parts = []
    for j, slot in enumerate(picked):
        scale = s / (s * s + lambdas[lam_index[slot]]) * live[slot].astype(F32)
        parts.append(total[j * BLK : (j + 1) * BLK, :] * scale)
    return parts


def products(where, outs, yt, us, wide, picked, held):
    for i, q in enumerate(where):
        wide[i].wait()
        total = jnp.dot(yt[...], us[i], preferred_element_type=F32)
        for j, part in enumerate(scaled(total, q, picked, *held)):
            outs[i][j][...] = part.astype(outs[i][j].dtype)


def start_kernel(lambdas_h, lam_index_h, live_h, sing_h, u, y, *rest):
    out_0, out_1, yt_out, lambdas, lam_index, live, sing, ys, us, sems = rest
    x, _, _, c = place()
    where = [quarter(name, x, c) for name in ("a", "opposite")]
    held = (lambdas, lam_index, live, sing)
    copies = [
        pltpu.make_async_copy(r, h, sems.at[i])
        for i, (r, h) in enumerate(zip((lambdas_h, lam_index_h, live_h, sing_h), held))
    ]
    whole = pltpu.make_async_copy(y, ys, sems.at[4])
    wide = [
        pltpu.make_async_copy(u.at[:, pl.ds(pl.multiple_of(q * Q, Q), Q)], us.at[i], sems.at[5 + i])
        for i, q in enumerate(where)
    ]
    for copy in copies + [whole] + wide:
        copy.start()
    for copy in copies:
        copy.wait()
    picked = slots(live)
    whole.wait()
    for j, slot in enumerate(picked):
        block = ys[:, pl.ds(pl.multiple_of(slot * BLK, BLK), BLK)]
        yt_out[j * BLK : (j + 1) * BLK, :] = block.T
    outs = [[out_0.at[i], out_1.at[i]] for i in range(2)]
    products(where, outs, yt_out, us, wide, picked, held)


def start_call(lambdas, lam_index, live, sing, u, y):
    return pl.pallas_call(
        start_kernel,
        out_shape=[jax.ShapeDtypeStruct((2, BLK, Q), BF16)] * 2
        + [jax.ShapeDtypeStruct((W, T), BF16)],
        in_specs=[HBM] * 6,
        out_specs=[VMEM] * 3,
        scratch_shapes=SMALL
        + [pltpu.VMEM((T, VD), BF16), pltpu.VMEM((2, T, Q), BF16), pltpu.SemaphoreType.DMA((7,))],
        compiler_params=pltpu.CompilerParams(vmem_limit_bytes=10 << 20),
        cost_estimate=pl.CostEstimate(
            flops=4 * W * T * Q, bytes_accessed=4 * T * Q, transcendentals=0
        ),
    )(*pin(lambdas, lam_index, live, sing, u, y))


def rest_kernel(lambdas_h, lam_index_h, live_h, sing_h, u, yt, *rest):
    outs, (lambdas, lam_index, live, sing, us, sems) = rest[:4], rest[4:]
    x, _, _, c = place()
    where = [quarter(name, x, c) for name in ("b", "own")]
    held = (lambdas, lam_index, live, sing)
    copies = [
        pltpu.make_async_copy(r, h, sems.at[i])
        for i, (r, h) in enumerate(zip((lambdas_h, lam_index_h, live_h, sing_h), held))
    ]
    wide = [
        pltpu.make_async_copy(u.at[:, pl.ds(pl.multiple_of(q * Q, Q), Q)], us.at[i], sems.at[4 + i])
        for i, q in enumerate(where)
    ]
    for copy in copies + wide:
        copy.start()
    for copy in copies:
        copy.wait()
    products(where, [outs[:2], outs[2:]], yt, us, wide, slots(live), held)


def rest_call(lambdas, lam_index, live, sing, u, yt):
    return pl.pallas_call(
        rest_kernel,
        out_shape=[jax.ShapeDtypeStruct((BLK, Q), F32)] * 4,
        in_specs=[HBM] * 5 + [VMEM],
        out_specs=[VMEM] * 4,
        scratch_shapes=SMALL + [pltpu.VMEM((2, T, Q), BF16), pltpu.SemaphoreType.DMA((6,))],
        compiler_params=pltpu.CompilerParams(vmem_limit_bytes=10 << 20),
        cost_estimate=pl.CostEstimate(
            flops=4 * W * T * Q, bytes_accessed=4 * T * Q, transcendentals=0
        ),
    )(*pin(lambdas, lam_index, live, sing, u), yt)


def row_kernel(a, b, c, d, out):
    for i, block in enumerate((a, b, c, d)):
        out[i] = block[...]


def row_call(*blocks):
    return pl.pallas_call(
        row_kernel,
        out_shape=jax.ShapeDtypeStruct((NY, Q, BLK), BF16),
        in_specs=[VMEM] * 4,
        out_specs=VMEM,
        compiler_params=pltpu.CompilerParams(vmem_limit_bytes=2 << 20),
        cost_estimate=pl.CostEstimate(
            flops=ROW_COST, bytes_accessed=4 * Q * Q, transcendentals=0
        ),
    )(*blocks)


def pass_kernel(*refs):
    pass


def hold(cost, *values):
    n = len(values)
    return pl.pallas_call(
        pass_kernel,
        out_shape=[jax.ShapeDtypeStruct(v.shape, v.dtype) for v in values],
        in_specs=[VMEM] * n,
        out_specs=[VMEM] * n,
        input_output_aliases={i: i for i in range(n)},
        compiler_params=pltpu.CompilerParams(vmem_limit_bytes=1 << 20),
        cost_estimate=pl.CostEstimate(flops=cost, bytes_accessed=1 << 20, transcendentals=0),
    )(*values)


CHUNK = 256


def block_of(distance):
    return jnp.where(distance == 3, 2, jnp.where(distance == 2, 3, distance))


def multiply(q, rows, shards, features):
    _, y, z0, c = place()
    back = (y - q + NY) % NY
    total = None
    for z in range(NZ):
        deep = (z0 - z + NZ) % NZ
        first = c * NY * NZ + block_of(deep) * NY + back
        second = (1 - c) * NY * NZ + block_of(back) * NZ + deep
        left = jnp.concatenate([shards[first, rows, :], shards[second, rows, :]], axis=1)
        columns = slice(z * NC * BLK, (z + 1) * NC * BLK)
        right = jnp.concatenate([f[:, columns] for f in features], axis=0)
        part = lax.dot_general(left, right, (((1,), (1,)), ((), ())), preferred_element_type=F32)
        total = part if total is None else total + part
    return total


def spread(out, rows, values, live):
    first, second = slots(live)
    left, right = values[:, :BLK], values[:, BLK:]
    for b in range(NB):
        block = jnp.where(first == b, left, right)
        block = jnp.where(live[b] > 0, block, jnp.zeros_like(block))
        out[rows, b * BLK : (b + 1) * BLK] = block.astype(out.dtype)


def last_kernel(shards, far_0, far_1, own_0, own_1, other_0, other_1, tests, *rest):
    packed, mine, to_a, to_b, opposite = rest
    x, _, _, c = place()
    for r in range(Q // CHUNK):
        rows = slice(r * CHUNK, (r + 1) * CHUNK)
        total = multiply(x, rows, shards, (own_0, own_1))
        total = total + multiply(quarter("b", x, c), rows, shards, (other_0, other_1))
        for i, name in enumerate(("a", "opposite")):
            total = total + multiply(
                quarter(name, x, c), rows, shards, (far_0.at[i], far_1.at[i])
            )
        total = total.astype(BF16)
        packed[rows, :] = total
    count = TEST // NX
    for name, out in (
        ("opposite", opposite),
        ("a", to_a),
        ("b", to_b),
        ("own", mine),
    ):
        q = quarter(name, x, c)
        part = tests[pl.ds(pl.multiple_of(q * count, count), count), :]
        out[...] = jnp.dot(part, packed[...], preferred_element_type=F32).astype(out.dtype)


def last_call(shards, far, near, tests):
    rows = TEST // NX
    return pl.pallas_call(
        last_kernel,
        out_shape=[
            jax.ShapeDtypeStruct((Q, W), BF16),
            jax.ShapeDtypeStruct((rows, W), F32),
            jax.ShapeDtypeStruct((rows, W), BF16),
            jax.ShapeDtypeStruct((rows, W), BF16),
            jax.ShapeDtypeStruct((rows, W), BF16),
        ],
        in_specs=[VMEM] * 8,
        out_specs=[VMEM] * 5,
        compiler_params=pltpu.CompilerParams(vmem_limit_bytes=8 << 20),
        cost_estimate=pl.CostEstimate(
            flops=4 * W * Q * Q, bytes_accessed=4 * Q * Q, transcendentals=0
        ),
    )(shards, *far, *near, tests)


def spread_kernel(live_h, packed, out, picks, live, sem):
    copy = pltpu.make_async_copy(live_h, live, sem)
    copy.start()
    copy.wait()
    chosen = slots(live)
    for i, slot in enumerate(chosen):
        for b in range(NB):
            here = jnp.where((slot == b) & (live[b] > 0), 1.0, 0.0)
            picks[i, :, b * BLK : (b + 1) * BLK] = jnp.full((8, BLK), here, F32)
    for r in range(Q // CHUNK):
        rows = slice(r * CHUNK, (r + 1) * CHUNK)
        spread(out, rows, packed[rows, :], live)


def spread_call(live, packed):
    return pl.pallas_call(
        spread_kernel,
        out_shape=[
            jax.ShapeDtypeStruct((Q, VD), BF16),
            jax.ShapeDtypeStruct((NS, 8, VD), F32),
        ],
        in_specs=[HBM, VMEM],
        out_specs=[VMEM] * 2,
        scratch_shapes=[pltpu.SMEM((NB,), jnp.int32), pltpu.SemaphoreType.DMA],
        compiler_params=pltpu.CompilerParams(vmem_limit_bytes=4 << 20),
        cost_estimate=pl.CostEstimate(
            flops=1 << 20, bytes_accessed=4 << 20, transcendentals=0
        ),
    )(*pin(live), packed)


def end_sum(picks, mine, *parts):
    total = mine
    for part in parts:
        total = total + part.astype(F32)
    left, right = (jnp.concatenate([h] * NB, axis=1) for h in jnp.split(total, 2, axis=1))
    first, second = (picks[i, :1, :] > 0 for i in range(NS))
    return jnp.where(first, left, jnp.where(second, right, 0.0)).astype(BF16)


def body(u_train, y_train, sing, lambdas, lam_index, live, v_basis, x_test):
    sing = sing.reshape(1, F)
    small = (lambdas, lam_index, live, sing)
    *p_send, yt = start_call(*small, u_train, y_train)
    come_0, come_1 = [send(p, PAIR_A) for p in p_send]
    near = [send(after(v_basis, yt), pairs) for pairs in FIRST]
    p_b0, p_b1, p_own0, p_own1 = rest_call(*small, u_train, yt)
    row = row_call(v_basis, *near)
    come_1 = after(come_1, row)
    sum_0 = (p_b0 + come_0[1].astype(F32)).astype(BF16)
    come_1 = after(come_1, sum_0)
    sum_1 = (p_b1 + come_1[1].astype(F32)).astype(BF16)
    from_0, from_b = send(sum_0, PAIR_B), send(sum_1, PAIR_B)
    ahead = [send(row, pairs) for pairs in SECOND[:2]]
    own_0 = (p_own0 + come_0[0].astype(F32) + from_0.astype(F32)).astype(BF16)
    across = send(after(row, own_0), SECOND[2])
    from_1 = after(from_b, own_0)
    own_1 = (p_own1 + come_1[0].astype(F32) + from_1.astype(F32)).astype(BF16)
    other_0, other_1 = send(own_0, PAIR_B), send(own_1, PAIR_B)
    both_0 = jnp.stack([own_0, other_0])
    other_1 = after(other_1, both_0)
    both_1 = jnp.stack([own_1, other_1])
    (far_0,) = hold(2000_000_000, send(both_0, PAIR_A))
    far = hold(100000_000_000, far_0, send(both_1, PAIR_A))
    pair = jnp.concatenate(after(ahead[:2], both_0))
    far_row = after(across, pair)
    early = jnp.concatenate([row, pair])
    early_other = send(early, SWAP)
    far_other = send(far_row, SWAP)
    shards = jnp.concatenate([early, far_row, early_other, far_other])
    packed, mine, to_a, to_b, opposite = last_call(shards, far, (own_0, own_1, other_0, other_1), x_test)
    weights, picks = spread_call(live, packed)
    predictions = end_sum(
        picks, mine, send(opposite, OPPOSITE), send(to_a, PAIR_A), send(to_b, PAIR_B)
    )
    return weights, predictions


def solution(mesh):
    placed = (
        P("tm", None),
        P("tm", "vox"),
        P(),
        P(),
        P("vox"),
        P("vox"),
        P("tm", "vox"),
        P(None, "tm"),
    )
    return jax.shard_map(
        body,
        mesh=mesh,
        in_specs=placed,
        out_specs=(P("tm", "vox"), P("tm", "vox")),
        check_vma=False,
    )
```
